128 devices in a mesh: view: 4 (over z_hi, core), rows: 32 (over y, x, z_lo).
Axes of the slice: x: 4, y: 4, z: 4 (z_hi: 2, z_lo: 2; z = z_hi * 2 + z_lo), core: 2. Of those that a mesh axis runs over, the one named last changes fastest.
Arguments:
- features: bfloat16 [12, 12, 256, 256, 128], P('view', None, 'rows'), may hold values from -6 to 6
- analysis_kernel: bfloat16 [5, 5, 128, 128], replicated, may hold values from -0.109375 to 0.109375
- norm_floor: float32 [128], replicated, may hold values from 0.3 to 3
- norm_mixing: float32 [128, 128], replicated, may hold values from 0 to 0.015625
- epipolar_kernel: bfloat16 [3, 3, 3, 128, 128], replicated, may hold values from -0.109375 to 0.109375
- epipolar_bias: float32 [128], replicated, may hold values from -3 to 3
Outputs:
- analysis: bfloat16 [12, 12, 128, 128, 128], P(None, None, ('rows', 'view'))
The draws below stay inside these ranges and needn't reach their ends.
All inputs are finite; a program needn't handle non-finite values.
Results may differ from the reference program's by a relative error of at most 0.007.
Values may be sent and summed in bfloat16 or wider, within the bound.
No kernel may reach another device: no remote copies, remote signals or barrier semaphores. Data moves between devices by JAX's collectives and lax.ppermute only.
A program may use at most 128 MiB of HBM per device.

```python
import math
import jax
import jax.numpy as jnp
from jax import lax

C = 128
ANG = 12
HIN = 256
WIN = 256


def levels(key, dims, pieces, low, high):
    def one(dim, parts):
        draws = jax.random.uniform(jax.random.fold_in(jax.random.fold_in(key, 6), dim), (parts,), jnp.float32, low / len(pieces), high / len(pieces))
        return jnp.repeat(jnp.exp(draws), dims[dim] // parts).reshape((-1,) + (1,) * (len(dims) - dim - 1))

    factor_of = one(*pieces[0])
    for cut in pieces[1:]:
        factor_of = factor_of * one(*cut)
    return factor_of


def gaussian(stream_key, extent, scale, bound, pieces=(), held_as=jnp.bfloat16):
    factor_of = levels(stream_key, extent, pieces, -0.22, 0.18) if pieces else 1.0
    values = jax.random.normal(stream_key, extent, jnp.float32) * scale * factor_of
    return jnp.minimum(jnp.maximum(values, -bound), bound).astype(held_as)


def setup_inputs(seed: int = 0) -> dict:
    keys = jax.random.split(jax.random.key(seed), 7)
    features = gaussian(keys[0], (ANG, ANG, HIN, WIN, C), 1.0, 6.0, ((0, 4), (2, 32)))
    analysis_kernel = gaussian(keys[1], (5, 5, C, C), (25 * C) ** -0.5, 0.109375)
    norm_floor = jnp.clip(jnp.exp(jax.random.uniform(keys[2], (C,), jnp.float32, math.log(0.3), math.log(3.0))), 0.3, 3.0)
    norm_mixing = jnp.clip(jax.random.uniform(keys[3], (C, C), jnp.float32, 0.0, 0.015625), 0.0, 0.015625)
    epipolar_kernel = gaussian(keys[4], (3, 3, 3, C, C), (27 * C) ** -0.5, 0.109375)
    epipolar_bias = gaussian(keys[5], (C,), 0.5, 3.0, (), jnp.float32)
    return dict(features=features, analysis_kernel=analysis_kernel, norm_floor=norm_floor, norm_mixing=norm_mixing, epipolar_kernel=epipolar_kernel, epipolar_bias=epipolar_bias)


def strided(view_block, kernel, pad_rows):
    return lax.conv_general_dilated(view_block, kernel, (2, 2), (pad_rows, (2, 2)), dimension_numbers=('NHWC', 'HWIO', 'NHWC'), preferred_element_type=jnp.float32)

def divisive(response, norm_floor, norm_mixing):
    energy = jnp.einsum('...c,cd->...d', response * response, norm_mixing, precision=lax.Precision.HIGHEST)
    return (response * lax.rsqrt(norm_floor + energy)).astype(jnp.bfloat16)

def epipolar(row_bands, kernel, bias):
    result = lax.conv_general_dilated(row_bands, kernel, (1, 1, 1), ((1, 1), (1, 1), (1, 1)), dimension_numbers=('DHNWC', 'DHWIO', 'DHNWC'), preferred_element_type=jnp.float32)
    return (result + bias).astype(jnp.bfloat16)

def reference(features, analysis_kernel, norm_floor, norm_mixing, epipolar_kernel, epipolar_bias):

    def per_row(view_block):
        return divisive(strided(view_block, analysis_kernel, (2, 2)), norm_floor, norm_mixing)
    coded_views = lax.map(per_row, features)
    return epipolar(coded_views, epipolar_kernel, epipolar_bias)
```

```python
import functools
import jax, jax.numpy as jnp
from jax import lax
from jax.experimental import pallas as pl
from jax.experimental.pallas import tpu as pltpu
from jax.sharding import PartitionSpec as P

bf16, f32 = jnp.bfloat16, jnp.float32

def shifted_sum(before, here, after, cols):
    rows = before.shape[0]
    place = lax.broadcasted_iota(jnp.int32, before.shape, 0) % cols
    down = jnp.where(place == 0, 0.0, pltpu.roll(before, 1, 0))
    up = jnp.where(place == cols - 1, 0.0, pltpu.roll(after, rows - 1, 0))
    return down + here + up

def conv_kernel(view_ref, x_ref, wm_ref, we_ref, own_ref, oth_ref, h1_ref, h2_ref, wide, ev, od):
    g, rows, wid, c = x_ref.shape[0], x_ref.shape[2], x_ref.shape[3], x_ref.shape[4]
    n = wid // 2
    m = g * n
    for v in range(g):
      for i in range(rows):
        wide[...] = x_ref[v, 0, i].astype(f32)
        ev[v, i] = wide[pl.ds(0, n, 2), :].astype(bf16)
        od[v, i] = wide[pl.ds(1, n, 2), :].astype(bf16)
    first = view_ref[0] < 2
    def block(ref, i):
        return ref[:, i].reshape(m, c)
    def main(lo, hi, a):
        lhs = jnp.concatenate([block(ref, i) for i in range(lo, hi) for ref in (ev, od)], axis=1)
        return jnp.dot(lhs, wm_ref[a * 2 * c:(a + hi - lo) * 2 * c, :], preferred_element_type=f32)
    def extra(lo, hi, a):
        lhs = jnp.concatenate([block(ev, i) for i in range(lo, hi)], axis=1)
        return jnp.dot(lhs, we_ref[a * c:(a + hi - lo) * c, :], preferred_element_type=f32)
    def row(mn, ex):
        return shifted_sum(mn[:, :c], mn[:, c:], ex, n).astype(bf16).reshape(g, n, c)
    pair = extra(0, 3, 4)
    up = row(main(0, 1, 4), pair[:, :c])
    r0 = row(main(0, 3, 2), pair[:, c:])
    pair = extra(4, 8, 0)
    r3 = row(main(4, 8, 0), pair[:, :c])
    dn = row(main(6, 8, 0), pair[:, c:])
    h1_ref[:, 0] = jnp.where(first, dn, up)
    h2_ref[:, 0] = jnp.where(first, up, dn)
    pair = extra(0, 7, 0)
    r1 = row(main(0, 5, 0), pair[:, :c])
    r2 = row(main(2, 7, 0), pair[:, c:])
    own_ref[0, :, 0] = jnp.where(first, r0, r2)
    own_ref[1, :, 0] = jnp.where(first, r1, r3)
    oth_ref[0, :, 0] = jnp.where(first, r2, r0)
    oth_ref[1, :, 0] = jnp.where(first, r3, r1)

def conv_weights(k):
    c = k.shape[2]
    main = jnp.stack([jnp.concatenate([k[:, 0], k[:, 2]], -1), jnp.concatenate([k[:, 1], k[:, 3]], -1)], 1)
    z = jnp.zeros((2,) + k.shape[2:], k.dtype)
    last = jnp.concatenate([jnp.concatenate([k[:, 4], z], 0), jnp.concatenate([z, k[:, 4]], 0)], -1)
    return main.reshape(-1, 2 * c), last.reshape(-1, 2 * c)

def conv_chunk(view, features, wm, we, lo, cv):
    U, V, H, W, C = features.shape
    n = W // 2
    spec = lambda lead: pl.BlockSpec(lead + (U, 1, n, C), lambda t, s: (0,) * len(lead) + (0, t, 0, 0))
    shp = lambda lead: jax.ShapeDtypeStruct(lead + (U, cv, n, C), bf16)
    full = lambda a: pl.BlockSpec(a.shape, lambda t, s: (0,) * a.ndim)
    return pl.pallas_call(
        conv_kernel,
        grid_spec=pltpu.PrefetchScalarGridSpec(
            num_scalar_prefetch=1, grid=(cv,),
            in_specs=[pl.BlockSpec((U, 1, H, W, C), lambda t, s: (0, lo + t, 0, 0, 0)), full(wm), full(we)],
            out_specs=[spec((2,)), spec((2,)), spec(()), spec(())],
            scratch_shapes=[pltpu.VMEM((W, C), f32), pltpu.VMEM((U, H, n, C), bf16), pltpu.VMEM((U, H, n, C), bf16)],
        ),
        out_shape=[shp((2,)), shp((2,)), shp(()), shp(())],
        compiler_params=pltpu.CompilerParams(vmem_limit_bytes=48 * 2**20),
        cost_estimate=pl.CostEstimate(flops=2 * cv * U * 4 * n * 25 * C * C, bytes_accessed=cv * U * (H * W + 6 * n) * C * 2, transcendentals=0),
        name="conv",
    )(view, features, wm, we)
def norm_kernel(place_ref, own_ref, oth_ref, h1_ref, h2_ref, floor_ref, mix_ref, mine_ref, give_ref):
    first = place_ref[0] < 2
    upper = place_ref[0] % 2 == 0
    g, n, c = h1_ref.shape[0], h1_ref.shape[2], h1_ref.shape[3]
    mix = mix_ref[...].astype(bf16)
    for j, (raw_ref, part_ref) in enumerate(((own_ref, h1_ref), (oth_ref, h2_ref))):
        part = part_ref[:, 0].reshape(g * n, c).astype(f32)
        coded = []
        for r in range(2):
            x = raw_ref[r, :, 0].reshape(g * n, c).astype(f32)
            x = x + jnp.where(first == (r == 0), part, 0.0)
            energy = jnp.dot((x * x).astype(bf16), mix, preferred_element_type=f32)
            coded.append((x * lax.rsqrt(floor_ref[...] + energy)).astype(bf16).reshape(g, n, c))
        mine_ref[j, :, 0] = jnp.where(upper, coded[0], coded[1])
        give_ref[j, :, 0] = jnp.where(upper, coded[1], coded[0])

def norm_chunk(place, own, oth, h1, h2, floor, mix):
    _, U, cv, n, C = own.shape
    spec = lambda lead: pl.BlockSpec(lead + (U, 1, n, C), lambda t, s: (0,) * len(lead) + (0, t, 0, 0))
    full = lambda a: pl.BlockSpec(a.shape, lambda t, s: (0,) * a.ndim)
    return pl.pallas_call(
        norm_kernel,
        grid_spec=pltpu.PrefetchScalarGridSpec(
            num_scalar_prefetch=1, grid=(cv,),
            in_specs=[spec((2,)), spec((2,)), spec(()), spec(()), full(floor), full(mix)],
            out_specs=[spec((2,)), spec((2,))],
        ),
        out_shape=[jax.ShapeDtypeStruct((2, U, cv, n, C), bf16)] * 2,
        compiler_params=pltpu.CompilerParams(vmem_limit_bytes=40 * 2**20),
        cost_estimate=pl.CostEstimate(flops=8 * cv * U * n * C * C, bytes_accessed=cv * U * 10 * n * C * 2, transcendentals=4 * cv * U * n * C),
        name="norm",
    )(place, own, oth, h1, h2, floor, mix)

def epi_kernel(pieces, v0, v1, has_prev, place_ref, *refs):
    k = len(pieces)
    srcs = refs[:2 * k]
    wm_ref, we_ref, bias_ref = refs[2 * k:2 * k + 3]
    rest = refs[2 * k + 3 + has_prev:]
    out_ref, cod, obuf, sem_in, sem_out = rest
    U = srcs[0].shape[1]
    n, c = cod.shape[2], cod.shape[3]
    V = out_ref.shape[1]
    total = out_ref.shape[0]
    nv = v1 - v0
    copies = []
    for p, (s0, s1, d0) in enumerate(pieces):
        for j, flip in enumerate((0, 2, 1, 3)):
            src = srcs[2 * p + j // 2]
            blk = place_ref[1 + j]
            cp = pltpu.make_async_copy(src.at[j % 2, :, s0:s1], cod.at[pl.ds(1 + U * blk, U), d0:d0 + s1 - s0], sem_in.at[4 * p + j])
            cp.start()
            copies.append(cp)
    edge = jnp.zeros((nv + 2, n, c), bf16)
    cod[0] = edge
    cod[total + 1] = edge
    if v0 == 0:
        cod[:, 0] = jnp.zeros((total + 2, n, c), bf16)
    if v1 == V:
        cod[:, nv + 1] = jnp.zeros((total + 2, n, c), bf16)
    for cp in copies:
        cp.wait()
    m = nv * n
    steps = total // 2
    def out_copy(t, slot):
        return pltpu.make_async_copy(obuf.at[slot], out_ref.at[pl.ds(2 * t, 2), v0:v1, 0], sem_out.at[slot])
    def step(t, carry):
        slot = lax.rem(t, 2)
        @pl.when(t >= 2)
        def _():
            out_copy(t - 2, slot).wait()
        def block(i, j):
            return cod[2 * t + i, j:j + nv].reshape(m, c)
        blocks = [[block(i, j) for j in range(3)] for i in range(4)]
        ex = jnp.dot(jnp.concatenate(sum(blocks, []), axis=1), we_ref[...], preferred_element_type=f32)
        for h in range(2):
            mn = jnp.dot(jnp.concatenate(sum(blocks[h:h + 3], []), axis=1), wm_ref[...], preferred_element_type=f32)
            res = shifted_sum(mn[:, :c], mn[:, c:], ex[:, h * c:(h + 1) * c], n) + bias_ref[...]
            obuf[slot, h] = res.astype(bf16).reshape(nv, n, c)
        out_copy(t, slot).start()
        return carry
    lax.fori_loop(0, steps, step, 0)
    for t in (steps - 2, steps - 1):
        out_copy(t, t % 2).wait()

def epi_weights(k):
    c = k.shape[3]
    main = jnp.concatenate([k[:, :, 0], k[:, :, 1]], -1).reshape(-1, 2 * c)
    z = jnp.zeros((1,) + k.shape[1:2] + k.shape[3:], k.dtype)
    last = jnp.concatenate([jnp.concatenate([k[:, :, 2], z], 0), jnp.concatenate([z, k[:, :, 2]], 0)], -1)
    return main, last.reshape(-1, 2 * c)

def epi_chunk(place, sources, spans, v0, v1, prev, wm, we, bias, total, V):
    used, pieces = [], []
    for (mine, flipped), (lo, hi) in zip(sources, spans):
        a, b = max(lo, v0 - 1), min(hi, v1 + 1)
        if a < b:
            used += [mine, flipped]
            pieces.append((a - lo, b - lo, a - (v0 - 1)))
    _, U, _, n, C = used[0].shape
    anyspec = pl.BlockSpec(memory_space=pl.ANY)
    full = lambda a: pl.BlockSpec(a.shape, lambda t, s: (0,) * a.ndim)
    nv = v1 - v0
    args = [place] + used + [wm, we, bias] + ([prev] if prev is not None else [])
    return pl.pallas_call(
        functools.partial(epi_kernel, tuple(pieces), v0, v1, int(prev is not None)),
        grid_spec=pltpu.PrefetchScalarGridSpec(
            num_scalar_prefetch=1, grid=(1,),
            in_specs=[anyspec] * len(used) + [full(wm), full(we), full(bias)] + [anyspec] * (prev is not None),
            out_specs=anyspec,
            scratch_shapes=[
                pltpu.VMEM((total + 2, nv + 2, n, C), bf16),
                pltpu.VMEM((2, 2, nv, n, C), bf16),
                pltpu.SemaphoreType.DMA((4 * len(pieces),)),
                pltpu.SemaphoreType.DMA((2,)),
            ],
        ),
        out_shape=jax.ShapeDtypeStruct((total, V, 1, n, C), bf16),
        input_output_aliases={len(args) - 1: 0} if prev is not None else {},
        compiler_params=pltpu.CompilerParams(vmem_limit_bytes=48 * 2**20),
        cost_estimate=pl.CostEstimate(flops=2 * total * nv * n * 27 * C * C, bytes_accessed=total * (2 * nv + 2) * n * C * 2, transcendentals=0),
        name="epi",
    )(*args)
CHUNKS = ((0, 6), (6, 12))

def shards(features, analysis_kernel, norm_floor, norm_mixing, epipolar_kernel, epipolar_bias):
    U, V = features.shape[:2]
    views, bands = lax.axis_size("view"), lax.axis_size("rows")
    total = U * views
    w = lax.axis_index("view")
    place = jnp.stack([w, w, w ^ 2, w ^ 1, w ^ 3]).astype(jnp.int32)
    wm, we = conv_weights(analysis_kernel)
    em, ee = epi_weights(epipolar_kernel)
    floor, bias = norm_floor[None], epipolar_bias[None]
    both = ("view", "rows")
    swap = [(v * bands + r, (v ^ 2) * bands + r) for v in range(views) for r in range(bands)]
    def hop(flip):
        pairs = []
        for v in range(views):
            step = 1 if (v < 2) != (flip > 0) else -1
            pairs += [(v * bands + r, (v ^ flip) * bands + r + step) for r in range(bands) if 0 <= r + step < bands]
        return pairs
    core = [(v, v ^ 1) for v in range(views)]
    sources = []
    out = None
    done = 0
    for i, (lo, hi) in enumerate(CHUNKS):
        own, oth, h1, h2 = conv_chunk(place, features, wm, we, lo, hi - lo)
        h1 = lax.ppermute(h1, both, hop(0))
        h2 = lax.ppermute(h2, both, hop(2))
        oth = lax.ppermute(oth, both, swap)
        mine, give = norm_chunk(place, own, oth, h1, h2, floor, norm_mixing)
        flipped = lax.ppermute(give, "view", core)
        sources.append((mine, flipped))
        upto = V if hi == V else hi - 1
        out = epi_chunk(place, sources, CHUNKS[:i + 1], done, upto, out, em, ee, bias, total, V)
        done = upto
    return out


def solution(mesh):
    in_specs = (P("view", None, "rows", None, None), P(), P(), P(), P(), P())
    out_specs = P(None, None, ("rows", "view"), None, None)
    return jax.shard_map(shards, mesh=mesh, in_specs=in_specs, out_specs=out_specs, check_vma=False)
```

```python
import functools
import jax, jax.numpy as jnp
from jax import lax
from jax.experimental import pallas as pl
from jax.experimental.pallas import tpu as pltpu
from jax.sharding import PartitionSpec as P

bf16, f32 = jnp.bfloat16, jnp.float32

SMALL = pl.CostEstimate(flops=1000, bytes_accessed=1000, transcendentals=0)


def shifted_sum(before, here, after, cols):
    rows = before.shape[0]
    place = lax.broadcasted_iota(jnp.int32, before.shape, 0) % cols
    down = jnp.where(place == 0, 0.0, pltpu.roll(before, 1, 0))
    up = jnp.where(place == cols - 1, 0.0, pltpu.roll(after, rows - 1, 0))
    return down + here + up

def split_columns(x_ref, v, i, wide, ev, od, at):
    n = wide.shape[0] // 2
    wide[...] = x_ref[v, 0, i].astype(f32)
    ev[v, at] = wide[pl.ds(0, n, 2), :].astype(bf16)
    od[v, at] = wide[pl.ds(1, n, 2), :].astype(bf16)


def main_weights(k_ref, wm_ref):
    c = k_ref.shape[2]
    for a in range(5):
        for p in range(2):
            for s in range(2):
                wm_ref[(2 * a + p) * c:(2 * a + p + 1) * c, s * c:(s + 1) * c] = k_ref[a, 2 * s + p]


def side_blocks(refs, blocks, m):
    return jnp.concatenate([refs[p][:, i].reshape(m, -1) for p, i in blocks], axis=1)


def halo_kernel(view_ref, top_ref, bottom_ref, k_ref, h1_ref, h2_ref, wide, ev, od, wm_ref, we_ref):
    g, wid, c = top_ref.shape[0], top_ref.shape[3], top_ref.shape[4]
    n = wid // 2
    m = g * n

    @pl.when(pl.program_id(0) == 0)
    def _():
        main_weights(k_ref, wm_ref)
        z = jnp.zeros((c, c), bf16)
        for r, (left, right) in enumerate(((4, None), (None, 0), (None, 1))):
            we_ref[r * c:(r + 1) * c, :c] = z if left is None else k_ref[left, 4]
            we_ref[r * c:(r + 1) * c, c:] = z if right is None else k_ref[right, 4]

    for v in range(g):
        split_columns(top_ref, v, 0, wide, ev, od, 0)
        split_columns(bottom_ref, v, 0, wide, ev, od, 1)
        split_columns(bottom_ref, v, 1, wide, ev, od, 2)
    first = view_ref[0] < 2
    refs = (ev, od)
    side = jnp.dot(side_blocks(refs, [(0, 0), (0, 1), (0, 2)], m), we_ref[...], preferred_element_type=f32)
    up = jnp.dot(side_blocks(refs, [(0, 0), (1, 0)], m), wm_ref[8 * c:, :], preferred_element_type=f32)
    up = shifted_sum(up[:, :c], up[:, c:], side[:, :c], n).astype(bf16).reshape(g, n, c)
    dn = jnp.dot(side_blocks(refs, [(0, 1), (1, 1), (0, 2), (1, 2)], m), wm_ref[:4 * c, :], preferred_element_type=f32)
    dn = shifted_sum(dn[:, :c], dn[:, c:], side[:, c:], n).astype(bf16).reshape(g, n, c)
    h1_ref[:, 0] = jnp.where(first, dn, up)
    h2_ref[:, 0] = jnp.where(first, up, dn)


def halo_sums(place, features, kernel):
    U, V, H, W, C = features.shape
    n = W // 2
    out = pl.BlockSpec((U, 1, n, C), lambda t, s: (0, t, 0, 0))
    return pl.pallas_call(
        halo_kernel,
        grid_spec=pltpu.PrefetchScalarGridSpec(
            num_scalar_prefetch=1, grid=(V,),
            in_specs=[
                pl.BlockSpec((U, 1, 1, W, C), lambda t, s: (0, t, 0, 0, 0)),
                pl.BlockSpec((U, 1, 2, W, C), lambda t, s: (0, t, H // 2 - 1, 0, 0)),
                pl.BlockSpec(kernel.shape, lambda t, s: (0, 0, 0, 0)),
            ],
            out_specs=[out, out],
            scratch_shapes=[
                pltpu.VMEM((W, C), f32), pltpu.VMEM((U, 3, n, C), bf16), pltpu.VMEM((U, 3, n, C), bf16),
                pltpu.VMEM((10 * C, 2 * C), bf16), pltpu.VMEM((3 * C, 2 * C), bf16),
            ],
        ),
        out_shape=[jax.ShapeDtypeStruct((U, V, n, C), bf16)] * 2,
        compiler_params=pltpu.CompilerParams(vmem_limit_bytes=48 * 2**20),
        cost_estimate=SMALL,
        name="halo",
    )(place, features, features, kernel)


def conv_kernel(view_ref, x_ref, k_ref, own_ref, oth_ref, wide, ev, od, wm_ref, we_ref):
    g, rows, wid, c = x_ref.shape[0], x_ref.shape[2], x_ref.shape[3], x_ref.shape[4]
    n = wid // 2
    m = g * n

    @pl.when(pl.program_id(0) == 0)
    def _():
        main_weights(k_ref, wm_ref)
        z = jnp.zeros((c, c), bf16)
        for j in range(7):
            we_ref[j * c:(j + 1) * c, :c] = k_ref[j, 4] if j < 5 else z
            we_ref[j * c:(j + 1) * c, c:] = k_ref[j - 2, 4] if j > 1 else z

    for v in range(g):
        for i in range(rows):
            split_columns(x_ref, v, i, wide, ev, od, i)
    first = view_ref[0] < 2
    refs = (ev, od)

    def main(lo, hi, a):
        lhs = side_blocks(refs, [(p, i) for i in range(lo, hi) for p in range(2)], m)
        return jnp.dot(lhs, wm_ref[a * 2 * c:(a + hi - lo) * 2 * c, :], preferred_element_type=f32)

    def side(lo, hi, a):
        lhs = side_blocks(refs, [(0, i) for i in range(lo, hi)], m)
        return jnp.dot(lhs, we_ref[a * c:(a + hi - lo) * c, :], preferred_element_type=f32)

    def row(mn, sd):
        return shifted_sum(mn[:, :c], mn[:, c:], sd, n).astype(bf16).reshape(g, n, c)

    pair = side(0, 5, 2)
    r0 = row(main(0, 3, 2), pair[:, :c])
    r1 = row(main(0, 5, 0), pair[:, c:])
    pair = side(2, 8, 0)
    r2 = row(main(2, 7, 0), pair[:, :c])
    r3 = row(main(4, 8, 0), pair[:, c:])
    own_ref[0, :, 0] = jnp.where(first, r0, r2)
    own_ref[1, :, 0] = jnp.where(first, r1, r3)
    oth_ref[0, :, 0] = jnp.where(first, r2, r0)
    oth_ref[1, :, 0] = jnp.where(first, r3, r1)


def conv_chunk(place, features, kernel, lo, cv):
    U, V, H, W, C = features.shape
    n = W // 2
    out = pl.BlockSpec((2, U, 1, n, C), lambda t, s: (0, 0, t, 0, 0))
    return pl.pallas_call(
        conv_kernel,
        grid_spec=pltpu.PrefetchScalarGridSpec(
            num_scalar_prefetch=1, grid=(cv,),
            in_specs=[
                pl.BlockSpec((U, 1, H, W, C), lambda t, s: (0, lo + t, 0, 0, 0)),
                pl.BlockSpec(kernel.shape, lambda t, s: (0, 0, 0, 0)),
            ],
            out_specs=[out, out],
            scratch_shapes=[
                pltpu.VMEM((W, C), f32), pltpu.VMEM((U, H, n, C), bf16), pltpu.VMEM((U, H, n, C), bf16),
                pltpu.VMEM((10 * C, 2 * C), bf16), pltpu.VMEM((7 * C, 2 * C), bf16),
            ],
        ),
        out_shape=[jax.ShapeDtypeStruct((2, U, cv, n, C), bf16)] * 2,
        compiler_params=pltpu.CompilerParams(vmem_limit_bytes=48 * 2**20),
        cost_estimate=SMALL,
        name="conv",
    )(place, features, kernel)


def norm_kernel(place_ref, own_ref, oth_ref, h1_ref, h2_ref, floor_ref, mix_ref, mine_ref, give0_ref, give1_ref):
    first = place_ref[0] < 2
    upper = place_ref[0] % 2 == 0
    g, n, c = h1_ref.shape[0], h1_ref.shape[2], h1_ref.shape[3]
    mix = mix_ref[...].astype(bf16)
    for j, (raw_ref, part_ref) in enumerate(((own_ref, h1_ref), (oth_ref, h2_ref))):
        part = part_ref[:, 0].reshape(g * n, c).astype(f32)
        coded = []
        for r in range(2):
            x = raw_ref[r, :, 0].reshape(g * n, c).astype(f32)
            x = x + jnp.where(first == (r == 0), part, 0.0)
            energy = jnp.dot((x * x).astype(bf16), mix, preferred_element_type=f32)
            coded.append((x * lax.rsqrt(floor_ref[...] + energy)).astype(bf16).reshape(g, n, c))
        mine_ref[j, :, 0] = jnp.where(upper, coded[0], coded[1])
        (give0_ref, give1_ref)[j][:, 0] = jnp.where(upper, coded[1], coded[0])

def norm_chunk(place, own, oth, h1, h2, floor, mix, lo):
    _, U, cv, n, C = own.shape
    spec = lambda lead, at=0: pl.BlockSpec(lead + (U, 1, n, C), lambda t, s: (0,) * len(lead) + (0, at + t, 0, 0))
    full = lambda a: pl.BlockSpec(a.shape, lambda t, s: (0,) * a.ndim)
    return pl.pallas_call(
        norm_kernel,
        grid_spec=pltpu.PrefetchScalarGridSpec(
            num_scalar_prefetch=1, grid=(cv,),
            in_specs=[spec((2,)), spec((2,)), spec((), lo), spec((), lo), full(floor), full(mix)],
            out_specs=[spec((2,)), spec(()), spec(())],
        ),
        out_shape=[jax.ShapeDtypeStruct((2, U, cv, n, C), bf16)] + [jax.ShapeDtypeStruct((U, cv, n, C), bf16)] * 2,
        compiler_params=pltpu.CompilerParams(vmem_limit_bytes=48 * 2**20),
        cost_estimate=SMALL,
        name="norm",
    )(place, own, oth, h1, h2, floor, mix)

def epi_kernel(pieces, v0, v1, has_prev, place_ref, *refs):
    k = len(pieces)
    srcs = refs[:3 * k]
    wm_ref, we_ref, bias_ref = refs[3 * k:3 * k + 3]
    rest = refs[3 * k + 3 + has_prev:]
    out_ref, cod, obuf, sem_in, sem_out = rest
    U = srcs[0].shape[1]
    n, c = cod.shape[2], cod.shape[3]
    V = out_ref.shape[1]
    total = out_ref.shape[0]
    nv = v1 - v0
    copies = []
    for p, (s0, s1, d0) in enumerate(pieces):
        for j in range(4):
            src = srcs[3 * p].at[j] if j < 2 else srcs[3 * p + j - 1]
            blk = place_ref[1 + j]
            cp = pltpu.make_async_copy(src.at[:, s0:s1], cod.at[pl.ds(1 + U * blk, U), d0:d0 + s1 - s0], sem_in.at[4 * p + j])
            cp.start()
            copies.append(cp)
    edge = jnp.zeros((nv + 2, n, c), bf16)
    cod[0] = edge
    cod[total + 1] = edge
    if v0 == 0:
        cod[:, 0] = jnp.zeros((total + 2, n, c), bf16)
    if v1 == V:
        cod[:, nv + 1] = jnp.zeros((total + 2, n, c), bf16)
    for cp in copies:
        cp.wait()
    m = nv * n
    steps = total // 2
    def out_copy(t, slot):
        return pltpu.make_async_copy(obuf.at[slot], out_ref.at[pl.ds(2 * t, 2), v0:v1, 0], sem_out.at[slot])
    def step(t, carry):
        slot = lax.rem(t, 2)
        @pl.when(t >= 2)
        def _():
            out_copy(t - 2, slot).wait()
        def block(i, j):
            return cod[2 * t + i, j:j + nv].reshape(m, c)
        blocks = [[block(i, j) for j in range(3)] for i in range(4)]
        ex = jnp.dot(jnp.concatenate(sum(blocks, []), axis=1), we_ref[...], preferred_element_type=f32)
        for h in range(2):
            mn = jnp.dot(jnp.concatenate(sum(blocks[h:h + 3], []), axis=1), wm_ref[...], preferred_element_type=f32)
            res = shifted_sum(mn[:, :c], mn[:, c:], ex[:, h * c:(h + 1) * c], n) + bias_ref[...]
            obuf[slot, h] = res.astype(bf16).reshape(nv, n, c)
        out_copy(t, slot).start()
        return carry
    lax.fori_loop(0, steps, step, 0)
    for t in (steps - 2, steps - 1):
        out_copy(t, t % 2).wait()

def epi_weights(k):
    c = k.shape[3]
    main = jnp.concatenate([k[:, :, 0], k[:, :, 1]], -1).reshape(-1, 2 * c)
    z = jnp.zeros((1,) + k.shape[1:2] + k.shape[3:], k.dtype)
    last = jnp.concatenate([jnp.concatenate([k[:, :, 2], z], 0), jnp.concatenate([z, k[:, :, 2]], 0)], -1)
    return main, last.reshape(-1, 2 * c)

def epi_chunk(place, sources, spans, v0, v1, prev, wm, we, bias, total, V):
    used, pieces = [], []
    for (mine, flipped), (lo, hi) in zip(sources, spans):
        a, b = max(lo, v0 - 1), min(hi, v1 + 1)
        if a < b:
            used += [mine, *flipped]
            pieces.append((a - lo, b - lo, a - (v0 - 1)))
    _, U, _, n, C = used[0].shape
    anyspec = pl.BlockSpec(memory_space=pl.ANY)
    full = lambda a: pl.BlockSpec(a.shape, lambda t, s: (0,) * a.ndim)
    nv = v1 - v0
    args = [place] + used + [wm, we, bias] + ([prev] if prev is not None else [])
    return pl.pallas_call(
        functools.partial(epi_kernel, tuple(pieces), v0, v1, int(prev is not None)),
        grid_spec=pltpu.PrefetchScalarGridSpec(
            num_scalar_prefetch=1, grid=(1,),
            in_specs=[anyspec] * len(used) + [full(wm), full(we), full(bias)] + [anyspec] * (prev is not None),
            out_specs=anyspec,
            scratch_shapes=[
                pltpu.VMEM((total + 2, nv + 2, n, C), bf16),
                pltpu.VMEM((2, 2, nv, n, C), bf16),
                pltpu.SemaphoreType.DMA((4 * len(pieces),)),
                pltpu.SemaphoreType.DMA((2,)),
            ],
        ),
        out_shape=jax.ShapeDtypeStruct((total, V, 1, n, C), bf16),
        input_output_aliases={len(args) - 1: 0} if prev is not None else {},
        compiler_params=pltpu.CompilerParams(vmem_limit_bytes=48 * 2**20),
        cost_estimate=SMALL,
        name="epi",
    )(*args)

CHUNKS = ((0, 5), (5, 9), (9, 12))


def shards(features, analysis_kernel, norm_floor, norm_mixing, epipolar_kernel, epipolar_bias):
    U, V = features.shape[:2]
    views, bands = lax.axis_size("view"), lax.axis_size("rows")
    total = U * views
    w = lax.axis_index("view")
    place = jnp.stack([w, w, w ^ 2, w ^ 1, w ^ 3]).astype(jnp.int32)
    em, ee = epi_weights(epipolar_kernel)
    floor, bias = norm_floor[None], epipolar_bias[None]
    both = ("view", "rows")
    swap = [(v * bands + r, (v ^ 2) * bands + r) for v in range(views) for r in range(bands)]
    def hop(flip):
        pairs = []
        for v in range(views):
            step = 1 if (v < 2) != (flip > 0) else -1
            pairs += [(v * bands + r, (v ^ flip) * bands + r + step) for r in range(bands) if 0 <= r + step < bands]
        return pairs
    core = [(v, v ^ 1) for v in range(views)]
    h1_sum, h2_sum = halo_sums(place, features, analysis_kernel)
    h1 = lax.ppermute(h1_sum, both, hop(0))
    h2 = lax.ppermute(h2_sum, both, hop(2))
    rows, sent = [], []
    turn, last = place, h1_sum
    for lo, hi in CHUNKS:
        turn, last = lax.optimization_barrier((turn, last))
        own, oth = conv_chunk(turn, features, analysis_kernel, lo, hi - lo)
        rows.append(own)
        sent.append(lax.ppermute(oth, both, swap))
        last = own
    sources = []
    out = None
    done = 0
    for i, (lo, hi) in enumerate(CHUNKS):
        own, oth = rows[i], sent[i]
        if out is None:
            oth, rows[-1] = lax.optimization_barrier((oth, rows[-1]))
        else:
            oth, out = lax.optimization_barrier((oth, out))
        mine, *give = norm_chunk(place, own, oth, h1, h2, floor, norm_mixing, lo)
        flipped = [lax.ppermute(g, "view", core) for g in give]
        sources.append((mine, flipped))
        upto = V if hi == V else hi - 1
        out = epi_chunk(place, sources, CHUNKS[:i + 1], done, upto, out, em, ee, bias, total, V)
        done = upto
    return out


def solution(mesh):
    in_specs = (P("view", None, "rows", None, None), P(), P(), P(), P(), P())
    out_specs = P(None, None, ("rows", "view"), None, None)
    return jax.shard_map(shards, mesh=mesh, in_specs=in_specs, out_specs=out_specs, check_vma=False)
```

```python
import functools
import jax, jax.numpy as jnp
from jax import lax
from jax.experimental import pallas as pl
from jax.experimental.pallas import tpu as pltpu
from jax.sharding import PartitionSpec as P

bf16, f32 = jnp.bfloat16, jnp.float32

SMALL = pl.CostEstimate(flops=1000, bytes_accessed=1000, transcendentals=0)


def shifted_sum(before, here, after, cols):
    rows = before.shape[0]
    place = lax.broadcasted_iota(jnp.int32, before.shape, 0) % cols
    down = jnp.where(place == 0, 0.0, pltpu.roll(before, 1, 0))
    up = jnp.where(place == cols - 1, 0.0, pltpu.roll(after, rows - 1, 0))
    return down + here + up

def split_columns(x_ref, v, i, wide, ev, od, at):
    n = wide.shape[1] // 2
    wide[at] = x_ref[v, i].astype(f32)
    ev[v, at] = wide[at, pl.ds(0, n, 2), :].astype(bf16)
    od[v, at] = wide[at, pl.ds(1, n, 2), :].astype(bf16)


def main_weights(k_ref, wm_ref):
    c = k_ref.shape[2]
    for a in range(5):
        for p in range(2):
            for s in range(2):
                wm_ref[(2 * a + p) * c:(2 * a + p + 1) * c, s * c:(s + 1) * c] = k_ref[a, 2 * s + p]


def side_blocks(refs, blocks, m):
    return jnp.concatenate([refs[p][:, i].reshape(m, -1) for p, i in blocks], axis=1)


def halo_kernel(view_ref, top_ref, bottom_ref, k_ref, h1_ref, h2_ref, wide, ev, od, wm_ref, we_ref):
    g, vs, wid, c = top_ref.shape[0], top_ref.shape[1], top_ref.shape[3], top_ref.shape[4]
    n = wid // 2
    m = g * n

    @pl.when(pl.program_id(0) == 0)
    def _():
        main_weights(k_ref, wm_ref)
        z = jnp.zeros((c, c), bf16)
        for r, (left, right) in enumerate(((4, None), (None, 0), (None, 1))):
            we_ref[r * c:(r + 1) * c, :c] = z if left is None else k_ref[left, 4]
            we_ref[r * c:(r + 1) * c, c:] = z if right is None else k_ref[right, 4]

    first = view_ref[0] < 2
    refs = (ev, od)
    for b in range(vs):
        for v in range(g):
            split_columns(top_ref.at[:, b], v, 0, wide, ev, od, 0)
            split_columns(bottom_ref.at[:, b], v, 0, wide, ev, od, 1)
            split_columns(bottom_ref.at[:, b], v, 1, wide, ev, od, 2)
        side = jnp.dot(side_blocks(refs, [(0, 0), (0, 1), (0, 2)], m), we_ref[...], preferred_element_type=f32)
        up = jnp.dot(side_blocks(refs, [(0, 0), (1, 0)], m), wm_ref[8 * c:, :], preferred_element_type=f32)
        up = shifted_sum(up[:, :c], up[:, c:], side[:, :c], n).astype(bf16).reshape(g, n, c)
        dn = jnp.dot(side_blocks(refs, [(0, 1), (1, 1), (0, 2), (1, 2)], m), wm_ref[:4 * c, :], preferred_element_type=f32)
        dn = shifted_sum(dn[:, :c], dn[:, c:], side[:, c:], n).astype(bf16).reshape(g, n, c)
        h1_ref[:, b] = jnp.where(first, dn, up)
        h2_ref[:, b] = jnp.where(first, up, dn)


def halo_sums(place, features, kernel):
    U, V, H, W, C = features.shape
    n = W // 2
    vs = HALO_STEP if V % HALO_STEP == 0 else 1
    out = pl.BlockSpec((U, vs, n, C), lambda t, s: (0, t, 0, 0))
    return pl.pallas_call(
        halo_kernel,
        grid_spec=pltpu.PrefetchScalarGridSpec(
            num_scalar_prefetch=1, grid=(V // vs,),
            in_specs=[
                pl.BlockSpec((U, vs, 1, W, C), lambda t, s: (0, t, 0, 0, 0)),
                pl.BlockSpec((U, vs, 2, W, C), lambda t, s: (0, t, H // 2 - 1, 0, 0)),
                pl.BlockSpec(memory_space=pltpu.VMEM),
            ],
            out_specs=[out, out],
            scratch_shapes=[
                pltpu.VMEM((3, W, C), f32), pltpu.VMEM((U, 3, n, C), bf16), pltpu.VMEM((U, 3, n, C), bf16),
                pltpu.VMEM((10 * C, 2 * C), bf16), pltpu.VMEM((3 * C, 2 * C), bf16),
            ],
        ),
        out_shape=[jax.ShapeDtypeStruct((U, V, n, C), bf16)] * 2,
        compiler_params=pltpu.CompilerParams(vmem_limit_bytes=48 * 2**20),
        cost_estimate=SMALL,
        name="halo",
    )(place, features, features, kernel)


def conv_kernel(starts, view_ref, x_ref, k_ref, *rest):
    outs, (wide, ev, od, wm_ref, we_ref) = rest[:-5], rest[-5:]
    g, rows, wid, c = x_ref.shape[0], x_ref.shape[2], x_ref.shape[3], x_ref.shape[4]
    n = wid // 2
    m = g * n

    @pl.when(pl.program_id(0) == 0)
    def _():
        main_weights(k_ref, wm_ref)
        z = jnp.zeros((c, c), bf16)
        for j in range(7):
            we_ref[j * c:(j + 1) * c, :c] = k_ref[j, 4] if j < 5 else z
            we_ref[j * c:(j + 1) * c, c:] = k_ref[j - 2, 4] if j > 1 else z

    for v in range(g):
        for i in range(rows):
            split_columns(x_ref.at[:, 0], v, i, wide, ev, od, i)
    first = view_ref[0] < 2
    refs = (ev, od)

    def main(lo, hi, a):
        lhs = side_blocks(refs, [(p, i) for i in range(lo, hi) for p in range(2)], m)
        return jnp.dot(lhs, wm_ref[a * 2 * c:(a + hi - lo) * 2 * c, :], preferred_element_type=f32)

    def side(lo, hi, a):
        lhs = side_blocks(refs, [(0, i) for i in range(lo, hi)], m)
        return jnp.dot(lhs, we_ref[a * c:(a + hi - lo) * c, :], preferred_element_type=f32)

    def row(mn, sd):
        return shifted_sum(mn[:, :c], mn[:, c:], sd, n).astype(bf16).reshape(g, n, c)

    def rows_of_step(own_ref, oth_ref):
        pair = side(0, 5, 2)
        r0 = row(main(0, 3, 2), pair[:, :c])
        r1 = row(main(0, 5, 0), pair[:, c:])
        pair = side(2, 8, 0)
        r2 = row(main(2, 7, 0), pair[:, :c])
        r3 = row(main(4, 8, 0), pair[:, c:])
        own_ref[0, :, 0] = jnp.where(first, r0, r2)
        own_ref[1, :, 0] = jnp.where(first, r1, r3)
        oth_ref[0, :, 0] = jnp.where(first, r2, r0)
        oth_ref[1, :, 0] = jnp.where(first, r3, r1)

    t = pl.program_id(0)
    for q, start in enumerate(starts):
        inside = t >= start
        if q + 1 < len(starts):
            inside = jnp.logical_and(inside, t < starts[q + 1])
        pl.when(inside)(functools.partial(rows_of_step, outs[2 * q], outs[2 * q + 1]))


def conv_chunks(place, features, kernel, spans):
    U, V, H, W, C = features.shape
    n = W // 2
    base = spans[0][0]
    starts = tuple(lo - base for lo, _ in spans)

    def out(lo, hi):
        return pl.BlockSpec((2, U, 1, n, C), lambda t, s: (0, 0, jnp.clip(t - (lo - base), 0, hi - lo - 1), 0, 0))

    return pl.pallas_call(
        functools.partial(conv_kernel, starts),
        grid_spec=pltpu.PrefetchScalarGridSpec(
            num_scalar_prefetch=1, grid=(spans[-1][1] - base,),
            in_specs=[
                pl.BlockSpec((U, 1, H, W, C), lambda t, s: (0, base + t, 0, 0, 0)),
                pl.BlockSpec(memory_space=pltpu.VMEM),
            ],
            out_specs=[out(*span) for span in spans for _ in range(2)],
            scratch_shapes=[
                pltpu.VMEM((H, W, C), f32), pltpu.VMEM((U, H, n, C), bf16), pltpu.VMEM((U, H, n, C), bf16),
                pltpu.VMEM((10 * C, 2 * C), bf16), pltpu.VMEM((7 * C, 2 * C), bf16),
            ],
        ),
        out_shape=[jax.ShapeDtypeStruct((2, U, hi - lo, n, C), bf16) for lo, hi in spans for _ in range(2)],
        compiler_params=pltpu.CompilerParams(vmem_limit_bytes=48 * 2**20),
        cost_estimate=SMALL,
        name="conv",
    )(place, features, kernel)


def norm_kernel(lo, place_ref, own_ref, oth_ref, h1_ref, h2_ref, floor_ref, mix_ref, mine_ref, give0_ref, give1_ref):
    first = place_ref[0] < 2
    upper = place_ref[0] % 2 == 0
    _, g, cv, n, c = own_ref.shape
    mix = mix_ref[...].astype(bf16)

    def step(v, carry):
        for j, (raw_ref, part_ref) in enumerate(((own_ref, h1_ref), (oth_ref, h2_ref))):
            part = part_ref[:, lo + v].reshape(g * n, c).astype(f32)
            coded = []
            for r in range(2):
                x = raw_ref[r, :, v].reshape(g * n, c).astype(f32)
                x = x + jnp.where(first == (r == 0), part, 0.0)
                energy = jnp.dot((x * x).astype(bf16), mix, preferred_element_type=f32)
                coded.append((x * lax.rsqrt(floor_ref[...] + energy)).astype(bf16).reshape(g, n, c))
            mine_ref[j, :, v] = jnp.where(upper, coded[0], coded[1])
            (give0_ref, give1_ref)[j][:, v] = jnp.where(upper, coded[1], coded[0])
        return carry

    lax.fori_loop(0, cv, step, 0)


def norm_chunk(place, own, oth, h1, h2, floor, mix, lo):
    _, U, cv, n, C = own.shape
    whole = pl.BlockSpec(memory_space=pltpu.VMEM)
    return pl.pallas_call(
        functools.partial(norm_kernel, lo),
        in_specs=[pl.BlockSpec(memory_space=pltpu.SMEM)] + [whole] * 6,
        out_specs=[whole] * 3,
        out_shape=[jax.ShapeDtypeStruct((2, U, cv, n, C), bf16)] + [jax.ShapeDtypeStruct((U, cv, n, C), bf16)] * 2,
        compiler_params=pltpu.CompilerParams(vmem_limit_bytes=16 * 2**20),
        cost_estimate=SMALL,
        name="norm",
    )(place, own, oth, h1, h2, floor, mix)


def epi_kernel(pieces, v0, v1, has_prev, place_ref, *refs):
    k = len(pieces)
    srcs = refs[:3 * k]
    wm_ref, we_ref, bias_ref = refs[3 * k:3 * k + 3]
    rest = refs[3 * k + 3 + has_prev:]
    out_ref, cod, obuf, sem_in, sem_out = rest
    U = srcs[0].shape[1]
    n, c = cod.shape[2], cod.shape[3]
    V = out_ref.shape[1]
    total = out_ref.shape[0]
    nv = v1 - v0
    for p, (s0, s1, d0) in enumerate(pieces):
        for j in range(4):
            src = srcs[3 * p].at[j] if j < 2 else srcs[3 * p + j - 1]
            blk = place_ref[1 + j]
            cp = pltpu.make_async_copy(src.at[:, s0:s1], cod.at[pl.ds(1 + U * blk, U), d0:d0 + s1 - s0], sem_in.at[4 * p + blk])
            cp.start()
    edge = jnp.zeros((nv + 2, n, c), bf16)
    cod[0] = edge
    cod[total + 1] = edge
    if v0 == 0:
        cod[:, 0] = jnp.zeros((total + 2, n, c), bf16)
    if v1 == V:
        cod[:, nv + 1] = jnp.zeros((total + 2, n, c), bf16)

    def arrived(b):
        for p, (s0, s1, d0) in enumerate(pieces):
            pltpu.make_async_copy(
                srcs[3 * p].at[0, :, s0:s1], cod.at[1 + U * b:1 + U * (b + 1), d0:d0 + s1 - s0], sem_in.at[4 * p + b]
            ).wait()
    m = nv * n
    steps = total // 2
    def out_copy(t, slot):
        return pltpu.make_async_copy(obuf.at[slot], out_ref.at[pl.ds(2 * t, 2), v0:v1, 0], sem_out.at[slot])
    def step(t, carry):
        slot = lax.rem(t, 2)
        for b in range(total // U):
            pl.when(t == max(0, -(-(U * b - 2) // 2)))(functools.partial(arrived, b))

        @pl.when(t >= 2)
        def _():
            out_copy(t - 2, slot).wait()
        def block(i, j):
            return cod[2 * t + i, j:j + nv].reshape(m, c)
        blocks = [[block(i, j) for j in range(3)] for i in range(4)]
        ex = jnp.dot(jnp.concatenate(sum(blocks, []), axis=1), we_ref[...], preferred_element_type=f32)
        for h in range(2):
            mn = jnp.dot(jnp.concatenate(sum(blocks[h:h + 3], []), axis=1), wm_ref[...], preferred_element_type=f32)
            res = shifted_sum(mn[:, :c], mn[:, c:], ex[:, h * c:(h + 1) * c], n) + bias_ref[...]
            obuf[slot, h] = res.astype(bf16).reshape(nv, n, c)
        out_copy(t, slot).start()
        return carry
    lax.fori_loop(0, steps, step, 0)
    for t in (steps - 2, steps - 1):
        out_copy(t, t % 2).wait()

def epi_weights(k):
    c = k.shape[3]
    main = jnp.concatenate([k[:, :, 0], k[:, :, 1]], -1).reshape(-1, 2 * c)
    z = jnp.zeros((1,) + k.shape[1:2] + k.shape[3:], k.dtype)
    last = jnp.concatenate([jnp.concatenate([k[:, :, 2], z], 0), jnp.concatenate([z, k[:, :, 2]], 0)], -1)
    return main, last.reshape(-1, 2 * c)

def epi_chunk(place, sources, spans, v0, v1, prev, wm, we, bias, total, V):
    used, pieces = [], []
    for (mine, flipped), (lo, hi) in zip(sources, spans):
        a, b = max(lo, v0 - 1), min(hi, v1 + 1)
        if a < b:
            used += [mine, *flipped]
            pieces.append((a - lo, b - lo, a - (v0 - 1)))
    _, U, _, n, C = used[0].shape
    anyspec = pl.BlockSpec(memory_space=pl.ANY)
    whole = pl.BlockSpec(memory_space=pltpu.VMEM)
    nv = v1 - v0
    args = [place] + used + [wm, we, bias] + ([prev] if prev is not None else [])
    return pl.pallas_call(
        functools.partial(epi_kernel, tuple(pieces), v0, v1, int(prev is not None)),
        grid_spec=pltpu.PrefetchScalarGridSpec(
            num_scalar_prefetch=1, grid=(1,),
            in_specs=[anyspec] * len(used) + [whole] * 3 + [anyspec] * (prev is not None),
            out_specs=anyspec,
            scratch_shapes=[
                pltpu.VMEM((total + 2, nv + 2, n, C), bf16),
                pltpu.VMEM((2, 2, nv, n, C), bf16),
                pltpu.SemaphoreType.DMA((4 * len(pieces),)),
                pltpu.SemaphoreType.DMA((2,)),
            ],
        ),
        out_shape=jax.ShapeDtypeStruct((total, V, 1, n, C), bf16),
        input_output_aliases={len(args) - 1: 0} if prev is not None else {},
        compiler_params=pltpu.CompilerParams(vmem_limit_bytes=24 * 2**20),
        cost_estimate=SMALL,
        name="epi",
    )(*args)


CHUNKS = ((0, 4), (4, 9), (9, 12))
HALO_STEP = 3


def shards(features, analysis_kernel, norm_floor, norm_mixing, epipolar_kernel, epipolar_bias):
    U, V = features.shape[:2]
    views, bands = lax.axis_size("view"), lax.axis_size("rows")
    total = U * views
    w = lax.axis_index("view")
    place = jnp.stack([w, w, w ^ 2, w ^ 1, w ^ 3]).astype(jnp.int32)
    em, ee = epi_weights(epipolar_kernel)
    floor, bias = norm_floor[None], epipolar_bias[None]
    both = ("view", "rows")
    swap = [(v * bands + r, (v ^ 2) * bands + r) for v in range(views) for r in range(bands)]
    def hop(flip):
        pairs = []
        for v in range(views):
            step = 1 if (v < 2) != (flip > 0) else -1
            pairs += [(v * bands + r, (v ^ flip) * bands + r + step) for r in range(bands) if 0 <= r + step < bands]
        return pairs
    core = [(v, v ^ 1) for v in range(views)]
    h1_sum, h2_sum = halo_sums(place, features, analysis_kernel)
    h1 = lax.ppermute(h1_sum, both, hop(0))
    h2 = lax.ppermute(h2_sum, both, hop(2))
    rows, sent = [], []
    turn, last = place, h1_sum
    for spans in (CHUNKS[:1], CHUNKS[1:]):
        turn, last = lax.optimization_barrier((turn, last))
        done = conv_chunks(turn, features, analysis_kernel, spans)
        for own, oth in zip(done[::2], done[1::2]):
            rows.append(own)
            sent.append(lax.ppermute(oth, both, swap))
        last = done[0]
    sources = []
    out = None
    done = 0
    for i, (lo, hi) in enumerate(CHUNKS):
        own, oth = rows[i], sent[i]
        if out is None:
            oth, rows[-1] = lax.optimization_barrier((oth, rows[-1]))
        else:
            oth, out = lax.optimization_barrier((oth, out))
        mine, *give = norm_chunk(place, own, oth, h1, h2, floor, norm_mixing, lo)
        flipped = [lax.ppermute(g, "view", core) for g in give]
        sources.append((mine, flipped))
        upto = V if hi == V else hi - 1
        out = epi_chunk(place, sources, CHUNKS[:i + 1], done, upto, out, em, ee, bias, total, V)
        done = upto
    return out


def solution(mesh):
    in_specs = (P("view", None, "rows", None, None), P(), P(), P(), P(), P())
    out_specs = P(None, None, ("rows", "view"), None, None)
    return jax.shard_map(shards, mesh=mesh, in_specs=in_specs, out_specs=out_specs, check_vma=False)
```

```python
import functools
import jax, jax.numpy as jnp
from jax import lax
from jax.experimental import pallas as pl
from jax.experimental.pallas import tpu as pltpu
from jax.sharding import PartitionSpec as P

bf16, f32 = jnp.bfloat16, jnp.float32

SMALL = pl.CostEstimate(flops=1000, bytes_accessed=1000, transcendentals=0)


def shifted_sum(before, here, after, cols):
    rows = before.shape[0]
    place = lax.broadcasted_iota(jnp.int32, before.shape, 0) % cols
    down = jnp.where(place == 0, 0.0, pltpu.roll(before, 1, 0))
    up = jnp.where(place == cols - 1, 0.0, pltpu.roll(after, rows - 1, 0))
    return down + here + up

def split_columns(x_ref, v, i, wide, ev, od, at):
    n = wide.shape[1] // 2
    wide[at] = x_ref[v, i].astype(f32)
    ev[v, at] = wide[at, pl.ds(0, n, 2), :].astype(bf16)
    od[v, at] = wide[at, pl.ds(1, n, 2), :].astype(bf16)


def main_weights(k_ref, wm_ref):
    c = k_ref.shape[2]
    for a in range(5):
        for p in range(2):
            for s in range(2):
                wm_ref[(2 * a + p) * c:(2 * a + p + 1) * c, s * c:(s + 1) * c] = k_ref[a, 2 * s + p]


def side_blocks(refs, blocks, m):
    return jnp.concatenate([refs[p][:, i].reshape(m, -1) for p, i in blocks], axis=1)


def halo_kernel(view_ref, top_ref, bottom_ref, k_ref, h1_ref, h2_ref, wide, ev, od, wm_ref, we_ref):
    g, vs, wid, c = top_ref.shape[0], top_ref.shape[1], top_ref.shape[3], top_ref.shape[4]
    n = wid // 2
    m = g * n

    @pl.when(pl.program_id(0) == 0)
    def _():
        main_weights(k_ref, wm_ref)
        z = jnp.zeros((c, c), bf16)
        for r, (left, right) in enumerate(((4, None), (None, 0), (None, 1))):
            we_ref[r * c:(r + 1) * c, :c] = z if left is None else k_ref[left, 4]
            we_ref[r * c:(r + 1) * c, c:] = z if right is None else k_ref[right, 4]

    first = view_ref[0] < 2
    refs = (ev, od)
    for b in range(vs):
        for v in range(g):
            split_columns(top_ref.at[:, b], v, 0, wide, ev, od, 0)
            split_columns(bottom_ref.at[:, b], v, 0, wide, ev, od, 1)
            split_columns(bottom_ref.at[:, b], v, 1, wide, ev, od, 2)
        side = jnp.dot(side_blocks(refs, [(0, 0), (0, 1), (0, 2)], m), we_ref[...], preferred_element_type=f32)
        up = jnp.dot(side_blocks(refs, [(0, 0), (1, 0)], m), wm_ref[8 * c:, :], preferred_element_type=f32)
        up = shifted_sum(up[:, :c], up[:, c:], side[:, :c], n).astype(bf16).reshape(g, n, c)
        dn = jnp.dot(side_blocks(refs, [(0, 1), (1, 1), (0, 2), (1, 2)], m), wm_ref[:4 * c, :], preferred_element_type=f32)
        dn = shifted_sum(dn[:, :c], dn[:, c:], side[:, c:], n).astype(bf16).reshape(g, n, c)
        h1_ref[:, b] = jnp.where(first, dn, up)
        h2_ref[:, b] = jnp.where(first, up, dn)


def halo_sums(place, features, kernel):
    U, V, H, W, C = features.shape
    n = W // 2
    vs = HALO_STEP if V % HALO_STEP == 0 else 1
    out = pl.BlockSpec((U, vs, n, C), lambda t, s: (0, t, 0, 0))
    return pl.pallas_call(
        halo_kernel,
        grid_spec=pltpu.PrefetchScalarGridSpec(
            num_scalar_prefetch=1, grid=(V // vs,),
            in_specs=[
                pl.BlockSpec((U, vs, 1, W, C), lambda t, s: (0, t, 0, 0, 0)),
                pl.BlockSpec((U, vs, 2, W, C), lambda t, s: (0, t, H // 2 - 1, 0, 0)),
                pl.BlockSpec(memory_space=pltpu.VMEM),
            ],
            out_specs=[out, out],
            scratch_shapes=[
                pltpu.VMEM((3, W, C), f32), pltpu.VMEM((U, 3, n, C), bf16), pltpu.VMEM((U, 3, n, C), bf16),
                pltpu.VMEM((10 * C, 2 * C), bf16), pltpu.VMEM((3 * C, 2 * C), bf16),
            ],
        ),
        out_shape=[jax.ShapeDtypeStruct((U, V, n, C), bf16)] * 2,
        compiler_params=pltpu.CompilerParams(vmem_limit_bytes=48 * 2**20),
        cost_estimate=SMALL,
        name="halo",
    )(place, features, features, kernel)


def conv_kernel(starts, view_ref, x_ref, k_ref, *rest):
    outs, (wide, ev, od, wm_ref, we_ref) = rest[:-5], rest[-5:]
    g, rows, wid, c = x_ref.shape[0], x_ref.shape[2], x_ref.shape[3], x_ref.shape[4]
    n = wid // 2
    m = g * n

    @pl.when(pl.program_id(0) == 0)
    def _():
        main_weights(k_ref, wm_ref)
        z = jnp.zeros((c, c), bf16)
        for j in range(7):
            we_ref[j * c:(j + 1) * c, :c] = k_ref[j, 4] if j < 5 else z
            we_ref[j * c:(j + 1) * c, c:] = k_ref[j - 2, 4] if j > 1 else z

    for v in range(g):
        for i in range(rows):
            split_columns(x_ref.at[:, 0], v, i, wide, ev, od, i)
    first = view_ref[0] < 2
    refs = (ev, od)

    def main(lo, hi, a):
        lhs = side_blocks(refs, [(p, i) for i in range(lo, hi) for p in range(2)], m)
        return jnp.dot(lhs, wm_ref[a * 2 * c:(a + hi - lo) * 2 * c, :], preferred_element_type=f32)

    def side(lo, hi, a):
        lhs = side_blocks(refs, [(0, i) for i in range(lo, hi)], m)
        return jnp.dot(lhs, we_ref[a * c:(a + hi - lo) * c, :], preferred_element_type=f32)

    def row(mn, sd):
        return shifted_sum(mn[:, :c], mn[:, c:], sd, n).astype(bf16).reshape(g, n, c)

    def rows_of_step(own_ref, oth_ref):
        pair = side(0, 5, 2)
        r0 = row(main(0, 3, 2), pair[:, :c])
        r1 = row(main(0, 5, 0), pair[:, c:])
        pair = side(2, 8, 0)
        r2 = row(main(2, 7, 0), pair[:, :c])
        r3 = row(main(4, 8, 0), pair[:, c:])
        own_ref[0, :, 0] = jnp.where(first, r0, r2)
        own_ref[1, :, 0] = jnp.where(first, r1, r3)
        oth_ref[0, :, 0] = jnp.where(first, r2, r0)
        oth_ref[1, :, 0] = jnp.where(first, r3, r1)

    t = pl.program_id(0)
    for q, start in enumerate(starts):
        inside = t >= start
        if q + 1 < len(starts):
            inside = jnp.logical_and(inside, t < starts[q + 1])
        pl.when(inside)(functools.partial(rows_of_step, outs[2 * q], outs[2 * q + 1]))


def conv_chunks(place, features, kernel, spans):
    U, V, H, W, C = features.shape
    n = W // 2
    base = spans[0][0]
    starts = tuple(lo - base for lo, _ in spans)

    def out(lo, hi):
        return pl.BlockSpec((2, U, 1, n, C), lambda t, s: (0, 0, jnp.clip(t - (lo - base), 0, hi - lo - 1), 0, 0))

    return pl.pallas_call(
        functools.partial(conv_kernel, starts),
        grid_spec=pltpu.PrefetchScalarGridSpec(
            num_scalar_prefetch=1, grid=(spans[-1][1] - base,),
            in_specs=[
                pl.BlockSpec((U, 1, H, W, C), lambda t, s: (0, base + t, 0, 0, 0)),
                pl.BlockSpec(memory_space=pltpu.VMEM),
            ],
            out_specs=[out(*span) for span in spans for _ in range(2)],
            scratch_shapes=[
                pltpu.VMEM((H, W, C), f32), pltpu.VMEM((U, H, n, C), bf16), pltpu.VMEM((U, H, n, C), bf16),
                pltpu.VMEM((10 * C, 2 * C), bf16), pltpu.VMEM((7 * C, 2 * C), bf16),
            ],
        ),
        out_shape=[jax.ShapeDtypeStruct((2, U, hi - lo, n, C), bf16) for lo, hi in spans for _ in range(2)],
        compiler_params=pltpu.CompilerParams(vmem_limit_bytes=48 * 2**20),
        cost_estimate=SMALL,
        name="conv",
    )(place, features, kernel)


def norm_kernel(lo, place_ref, own_ref, oth_ref, h1_ref, h2_ref, floor_ref, mix_ref, mine_ref, give0_ref, give1_ref):
    first = place_ref[0] < 2
    upper = place_ref[0] % 2 == 0
    _, g, cv, n, c = own_ref.shape
    mix = mix_ref[...].astype(bf16)

    def step(v, carry):
        for j, (raw_ref, part_ref) in enumerate(((own_ref, h1_ref), (oth_ref, h2_ref))):
            part = part_ref[:, lo + v].reshape(g * n, c).astype(f32)
            coded = []
            for r in range(2):
                x = raw_ref[r, :, v].reshape(g * n, c).astype(f32)
                x = x + jnp.where(first == (r == 0), part, 0.0)
                energy = jnp.dot((x * x).astype(bf16), mix, preferred_element_type=f32)
                coded.append((x * lax.rsqrt(floor_ref[...] + energy)).astype(bf16).reshape(g, n, c))
            mine_ref[j, :, v] = jnp.where(upper, coded[0], coded[1])
            (give0_ref, give1_ref)[j][:, v] = jnp.where(upper, coded[1], coded[0])
        return carry

    lax.fori_loop(0, cv, step, 0)


def norm_chunk(place, own, oth, h1, h2, floor, mix, lo):
    _, U, cv, n, C = own.shape
    whole = pl.BlockSpec(memory_space=pltpu.VMEM)
    return pl.pallas_call(
        functools.partial(norm_kernel, lo),
        in_specs=[pl.BlockSpec(memory_space=pltpu.SMEM)] + [whole] * 6,
        out_specs=[whole] * 3,
        out_shape=[jax.ShapeDtypeStruct((2, U, cv, n, C), bf16)] + [jax.ShapeDtypeStruct((U, cv, n, C), bf16)] * 2,
        compiler_params=pltpu.CompilerParams(vmem_limit_bytes=16 * 2**20),
        cost_estimate=SMALL,
        name="norm",
    )(place, own, oth, h1, h2, floor, mix)


def epi_kernel(pieces, v0, v1, has_prev, place_ref, *refs):
    k = len(pieces)
    srcs = refs[:3 * k]
    wm_ref, we_ref, bias_ref = refs[3 * k:3 * k + 3]
    rest = refs[3 * k + 3 + has_prev:]
    out_ref, cod, obuf, sem_in, sem_out = rest
    U = srcs[0].shape[1]
    n, c = cod.shape[2], cod.shape[3]
    V = out_ref.shape[1]
    total = out_ref.shape[0]
    nv = v1 - v0
    for p, (s0, s1, d0) in enumerate(pieces):
        for j in range(4):
            src = srcs[3 * p].at[j] if j < 2 else srcs[3 * p + j - 1]
            blk = place_ref[1 + j]
            cp = pltpu.make_async_copy(src.at[:, s0:s1], cod.at[pl.ds(1 + U * blk, U), d0:d0 + s1 - s0], sem_in.at[4 * p + blk])
            cp.start()
    edge = jnp.zeros((nv + 2, n, c), bf16)
    cod[0] = edge
    cod[total + 1] = edge
    if v0 == 0:
        cod[:, 0] = jnp.zeros((total + 2, n, c), bf16)
    if v1 == V:
        cod[:, nv + 1] = jnp.zeros((total + 2, n, c), bf16)

    def arrived(b):
        for p, (s0, s1, d0) in enumerate(pieces):
            pltpu.make_async_copy(
                srcs[3 * p].at[0, :, s0:s1], cod.at[1 + U * b:1 + U * (b + 1), d0:d0 + s1 - s0], sem_in.at[4 * p + b]
            ).wait()
    m = nv * n
    steps = total // 2
    def out_copy(t, slot):
        return pltpu.make_async_copy(obuf.at[slot], out_ref.at[pl.ds(2 * t, 2), v0:v1, 0], sem_out.at[slot])
    def step(t, carry):
        slot = lax.rem(t, 2)
        for b in range(total // U):
            pl.when(t == max(0, -(-(U * b - 2) // 2)))(functools.partial(arrived, b))

        @pl.when(t >= 2)
        def _():
            out_copy(t - 2, slot).wait()
        def block(i, j):
            return cod[2 * t + i, j:j + nv].reshape(m, c)
        blocks = [[block(i, j) for j in range(3)] for i in range(4)]
        ex = jnp.dot(jnp.concatenate(sum(blocks, []), axis=1), we_ref[...], preferred_element_type=f32)
        for h in range(2):
            mn = jnp.dot(jnp.concatenate(sum(blocks[h:h + 3], []), axis=1), wm_ref[...], preferred_element_type=f32)
            res = shifted_sum(mn[:, :c], mn[:, c:], ex[:, h * c:(h + 1) * c], n) + bias_ref[...]
            obuf[slot, h] = res.astype(bf16).reshape(nv, n, c)
        out_copy(t, slot).start()
        return carry
    lax.fori_loop(0, steps, step, 0)
    for t in (steps - 2, steps - 1):
        out_copy(t, t % 2).wait()

def epi_weights(k):
    c = k.shape[3]
    main = jnp.concatenate([k[:, :, 0], k[:, :, 1]], -1).reshape(-1, 2 * c)
    z = jnp.zeros((1,) + k.shape[1:2] + k.shape[3:], k.dtype)
    last = jnp.concatenate([jnp.concatenate([k[:, :, 2], z], 0), jnp.concatenate([z, k[:, :, 2]], 0)], -1)
    return main, last.reshape(-1, 2 * c)

def epi_chunk(place, sources, spans, v0, v1, prev, wm, we, bias, total, V):
    used, pieces = [], []
    for (mine, flipped), (lo, hi) in zip(sources, spans):
        a, b = max(lo, v0 - 1), min(hi, v1 + 1)
        if a < b:
            used += [mine, *flipped]
            pieces.append((a - lo, b - lo, a - (v0 - 1)))
    _, U, _, n, C = used[0].shape
    anyspec = pl.BlockSpec(memory_space=pl.ANY)
    whole = pl.BlockSpec(memory_space=pltpu.VMEM)
    nv = v1 - v0
    args = [place] + used + [wm, we, bias] + ([prev] if prev is not None else [])
    return pl.pallas_call(
        functools.partial(epi_kernel, tuple(pieces), v0, v1, int(prev is not None)),
        grid_spec=pltpu.PrefetchScalarGridSpec(
            num_scalar_prefetch=1, grid=(1,),
            in_specs=[anyspec] * len(used) + [whole] * 3 + [anyspec] * (prev is not None),
            out_specs=anyspec,
            scratch_shapes=[
                pltpu.VMEM((total + 2, nv + 2, n, C), bf16),
                pltpu.VMEM((2, 2, nv, n, C), bf16),
                pltpu.SemaphoreType.DMA((4 * len(pieces),)),
                pltpu.SemaphoreType.DMA((2,)),
            ],
        ),
        out_shape=jax.ShapeDtypeStruct((total, V, 1, n, C), bf16),
        input_output_aliases={len(args) - 1: 0} if prev is not None else {},
        compiler_params=pltpu.CompilerParams(vmem_limit_bytes=24 * 2**20),
        cost_estimate=SMALL,
        name="epi",
    )(*args)


CHUNKS = ((0, 4), (4, 9), (9, 12))
HALO_STEP = 3


def shards(features, analysis_kernel, norm_floor, norm_mixing, epipolar_kernel, epipolar_bias):
    U, V = features.shape[:2]
    views, bands = lax.axis_size("view"), lax.axis_size("rows")
    total = U * views
    w = lax.axis_index("view")
    place = jnp.stack([w, w, w ^ 2, w ^ 1, w ^ 3]).astype(jnp.int32)
    em, ee = epi_weights(epipolar_kernel)
    floor, bias = norm_floor[None], epipolar_bias[None]
    both = ("view", "rows")
    swap = [(v * bands + r, (v ^ 2) * bands + r) for v in range(views) for r in range(bands)]
    def hop(flip):
        pairs = []
        for v in range(views):
            step = 1 if (v < 2) != (flip > 0) else -1
            pairs += [(v * bands + r, (v ^ flip) * bands + r + step) for r in range(bands) if 0 <= r + step < bands]
        return pairs
    core = [(v, v ^ 1) for v in range(views)]
    h1_sum, h2_sum = halo_sums(place, features, analysis_kernel)
    h1 = lax.ppermute(h1_sum, both, hop(0))
    h2 = lax.ppermute(h2_sum, both, hop(2))
    rows, sent = [], []
    turn, last = place, h1_sum
    for spans in (CHUNKS[:1], CHUNKS[1:]):
        turn, last = lax.optimization_barrier((turn, last))
        done = conv_chunks(turn, features, analysis_kernel, spans)
        for own, oth in zip(done[::2], done[1::2]):
            rows.append(own)
            sent.append(oth)
        last = done[0]
    sent[0] = lax.ppermute(sent[0], both, swap)
    sent[1], h1, h2 = lax.optimization_barrier((sent[1], h1, h2))
    sent[1] = lax.ppermute(sent[1], both, swap)
    sources = []
    out = None
    done = 0
    for i, (lo, hi) in enumerate(CHUNKS):
        own, oth = rows[i], sent[i]
        if out is None:
            oth, rows[-1] = lax.optimization_barrier((oth, rows[-1]))
        else:
            oth, out = lax.optimization_barrier((oth, out))
        mine, *give = norm_chunk(place, own, oth, h1, h2, floor, norm_mixing, lo)
        flipped = [lax.ppermute(g, "view", core) for g in give]
        sources.append((mine, flipped))
        upto = V if hi == V else hi - 1
        out = epi_chunk(place, sources, CHUNKS[:i + 1], done, upto, out, em, ee, bias, total, V)
        done = upto
        if i + 2 < len(CHUNKS):
            later, out = lax.optimization_barrier((sent[i + 2], out))
            sent[i + 2] = lax.ppermute(later, both, swap)
    return out


def solution(mesh):
    in_specs = (P("view", None, "rows", None, None), P(), P(), P(), P(), P())
    out_specs = P(None, None, ("rows", "view"), None, None)
    return jax.shard_map(shards, mesh=mesh, in_specs=in_specs, out_specs=out_specs, check_vma=False)
```

```python
import functools
import jax, jax.numpy as jnp
from jax import lax
from jax.experimental import pallas as pl
from jax.experimental.pallas import tpu as pltpu
from jax.sharding import PartitionSpec as P

bf16, f32 = jnp.bfloat16, jnp.float32

SMALL = pl.CostEstimate(flops=1000, bytes_accessed=1000, transcendentals=0)


def shifted_sum(before, here, after, cols):
    rows = before.shape[0]
    place = lax.broadcasted_iota(jnp.int32, before.shape, 0) % cols
    down = jnp.where(place == 0, 0.0, pltpu.roll(before, 1, 0))
    up = jnp.where(place == cols - 1, 0.0, pltpu.roll(after, rows - 1, 0))
    return down + here + up

def split_columns(x_ref, v, i, wide, ev, od, at):
    n = wide.shape[1] // 2
    wide[at] = x_ref[v, i].astype(f32)
    ev[v, at] = wide[at, pl.ds(0, n, 2), :].astype(bf16)
    od[v, at] = wide[at, pl.ds(1, n, 2), :].astype(bf16)


def main_weights(k_ref, wm_ref):
    c = k_ref.shape[2]
    for a in range(5):
        for p in range(2):
            for s in range(2):
                wm_ref[(2 * a + p) * c:(2 * a + p + 1) * c, s * c:(s + 1) * c] = k_ref[a, 2 * s + p]


def side_blocks(refs, blocks, m):
    return jnp.concatenate([refs[p][:, i].reshape(m, -1) for p, i in blocks], axis=1)


def halo_kernel(x_ref, k_ref, h1_ref, h2_ref, wm_ref, we_ref, top, bottom, kern, wide, ev, od, sems):
    g, views, _, wid, c = top.shape
    rows = x_ref.shape[2]
    n = wid // 2
    m = g * n
    weights = pltpu.make_async_copy(k_ref, kern, sems.at[2 * views])
    weights.start()

    def pieces(b):
        return (
            pltpu.make_async_copy(x_ref.at[:, b, 0:1], top.at[:, b], sems.at[2 * b]),
            pltpu.make_async_copy(x_ref.at[:, b, rows - 2:rows], bottom.at[:, b], sems.at[2 * b + 1]),
        )

    for b in range(views):
        for piece in pieces(b):
            piece.start()
    weights.wait()
    main_weights(kern, wm_ref)
    z = jnp.zeros((c, c), bf16)
    for j in range(7):
        we_ref[j * c:(j + 1) * c, :c] = kern[j, 4] if j < 5 else z
        we_ref[j * c:(j + 1) * c, c:] = kern[j - 2, 4] if j > 1 else z
    first = lax.axis_index("view") < 2
    refs = (ev, od)

    def step(b, carry):
        for piece in pieces(b):
            piece.wait()
        for v in range(g):
            split_columns(top.at[:, b], v, 0, wide, ev, od, 0)
            split_columns(bottom.at[:, b], v, 0, wide, ev, od, 1)
            split_columns(bottom.at[:, b], v, 1, wide, ev, od, 2)
        up = jnp.dot(side_blocks(refs, [(0, 0), (1, 0)], m), wm_ref[8 * c:, :], preferred_element_type=f32)
        side = jnp.dot(side_blocks(refs, [(0, 0)], m), we_ref[4 * c:5 * c, :c], preferred_element_type=f32)
        up = shifted_sum(up[:, :c], up[:, c:], side, n).astype(bf16).reshape(g, n, c)
        dn = jnp.dot(side_blocks(refs, [(0, 1), (1, 1), (0, 2), (1, 2)], m), wm_ref[:4 * c, :], preferred_element_type=f32)
        side = jnp.dot(side_blocks(refs, [(0, 1), (0, 2)], m), we_ref[:2 * c, :c], preferred_element_type=f32)
        dn = shifted_sum(dn[:, :c], dn[:, c:], side, n).astype(bf16).reshape(g, n, c)
        h1_ref[:, b] = jnp.where(first, dn, up)
        h2_ref[:, b] = jnp.where(first, up, dn)
        return carry

    lax.fori_loop(0, views, step, 0)


def halo_sums(features, kernel):
    U, V, H, W, C = features.shape
    n = W // 2
    whole = pl.BlockSpec(memory_space=pltpu.VMEM)
    return pl.pallas_call(
        halo_kernel,
        in_specs=[pl.BlockSpec(memory_space=pl.ANY)] * 2,
        out_specs=[whole] * 4,
        scratch_shapes=[
            pltpu.VMEM((U, V, 1, W, C), bf16), pltpu.VMEM((U, V, 2, W, C), bf16), pltpu.VMEM(kernel.shape, bf16),
            pltpu.VMEM((3, W, C), f32), pltpu.VMEM((U, 3, n, C), bf16), pltpu.VMEM((U, 3, n, C), bf16),
            pltpu.SemaphoreType.DMA((2 * V + 1,)),
        ],
        out_shape=[jax.ShapeDtypeStruct((U, V, n, C), bf16)] * 2
        + [jax.ShapeDtypeStruct((taps * C, 2 * C), bf16) for taps in (10, 7)],
        compiler_params=pltpu.CompilerParams(vmem_limit_bytes=57 * 2**20),
        cost_estimate=SMALL,
        name="halo",
    )(features, kernel)


def conv_kernel(base, starts, x_ref, wm_ref, we_ref, *rest):
    outs, (xs, wide, ev, od, sems) = rest[:-5], rest[-5:]
    count, g, rows, wid, c = xs.shape
    n = wid // 2
    m = g * n

    def fetch(b):
        return pltpu.make_async_copy(x_ref.at[:, base + b], xs.at[b], sems.at[b])

    for b in range(count):
        fetch(b).start()
    first = lax.axis_index("view") < 2
    refs = (ev, od)

    def main(lo, hi, a):
        lhs = side_blocks(refs, [(p, i) for i in range(lo, hi) for p in range(2)], m)
        return jnp.dot(lhs, wm_ref[a * 2 * c:(a + hi - lo) * 2 * c, :], preferred_element_type=f32)

    def side(lo, hi, a):
        lhs = side_blocks(refs, [(0, i) for i in range(lo, hi)], m)
        return jnp.dot(lhs, we_ref[a * c:(a + hi - lo) * c, :], preferred_element_type=f32)

    def row(mn, sd):
        return shifted_sum(mn[:, :c], mn[:, c:], sd, n).astype(bf16).reshape(g, n, c)

    def step(own_ref, oth_ref, start, b, carry):
        fetch(b).wait()
        for v in range(g):
            for i in range(rows):
                split_columns(xs.at[b], v, i, wide, ev, od, i)
        at = b - start
        pair = side(0, 5, 2)
        r0 = row(main(0, 3, 2), pair[:, :c])
        r1 = row(main(0, 5, 0), pair[:, c:])
        pair = side(2, 8, 0)
        r2 = row(main(2, 7, 0), pair[:, :c])
        r3 = row(main(4, 8, 0), pair[:, c:])
        own_ref[0, :, at] = jnp.where(first, r0, r2)
        own_ref[1, :, at] = jnp.where(first, r1, r3)
        oth_ref[0, :, at] = jnp.where(first, r2, r0)
        oth_ref[1, :, at] = jnp.where(first, r3, r1)
        return carry

    for q, start in enumerate(starts):
        end = starts[q + 1] if q + 1 < len(starts) else count
        lax.fori_loop(start, end, functools.partial(step, outs[2 * q], outs[2 * q + 1], start), 0)


def conv_chunks(features, wm, we, spans):
    U, V, H, W, C = features.shape
    n = W // 2
    base = spans[0][0]
    starts = tuple(lo - base for lo, _ in spans)

    count = spans[-1][1] - base
    whole = pl.BlockSpec(memory_space=pltpu.VMEM)
    return pl.pallas_call(
        functools.partial(conv_kernel, base, starts),
        in_specs=[pl.BlockSpec(memory_space=pl.ANY), whole, whole],
        out_specs=[whole] * (2 * len(spans)),
        scratch_shapes=[
            pltpu.VMEM((count, U, H, W, C), bf16),
            pltpu.VMEM((H, W, C), f32), pltpu.VMEM((U, H, n, C), bf16), pltpu.VMEM((U, H, n, C), bf16),
            pltpu.SemaphoreType.DMA((count,)),
        ],
        out_shape=[jax.ShapeDtypeStruct((2, U, hi - lo, n, C), bf16) for lo, hi in spans for _ in range(2)],
        compiler_params=pltpu.CompilerParams(vmem_limit_bytes=46 * 2**20),
        cost_estimate=SMALL,
        name="conv",
    )(features, wm, we)


def norm_kernel(lo, own_ref, oth_ref, h1_ref, h2_ref, floor_ref, mix_ref, mine_ref, *give_refs):
    place = lax.axis_index("view")
    first = place < 2
    upper = place % 2 == 0
    _, g, cv, n, c = own_ref.shape
    mix = mix_ref[...].astype(bf16)

    def step(v, carry):
        for j, (raw_ref, part_ref) in enumerate(((own_ref, h1_ref), (oth_ref, h2_ref))):
            part = part_ref[:, lo + v].reshape(g * n, c).astype(f32)
            coded = []
            for r in range(2):
                x = raw_ref[r, :, v].reshape(g * n, c).astype(f32)
                x = x + jnp.where(first == (r == 0), part, 0.0)
                energy = jnp.dot((x * x).astype(bf16), mix, preferred_element_type=f32)
                coded.append((x * lax.rsqrt(floor_ref[...] + energy)).astype(bf16).reshape(g, n, c))
            mine_ref[j, :, v] = jnp.where(upper, coded[0], coded[1])
            give = give_refs[j] if len(give_refs) > 1 else give_refs[0].at[j]
            give[:, v] = jnp.where(upper, coded[1], coded[0])
        return carry

    lax.fori_loop(0, cv, step, 0)


def norm_chunk(own, oth, h1, h2, floor, mix, lo, parts):
    _, U, cv, n, C = own.shape
    whole = pl.BlockSpec(memory_space=pltpu.VMEM)
    return pl.pallas_call(
        functools.partial(norm_kernel, lo),
        in_specs=[whole] * 6,
        out_specs=[whole] * (1 + parts),
        out_shape=[jax.ShapeDtypeStruct((2, U, cv, n, C), bf16)]
        + [jax.ShapeDtypeStruct((2,) * (2 - parts) + (U, cv, n, C), bf16)] * parts,
        compiler_params=pltpu.CompilerParams(vmem_limit_bytes=16 * 2**20),
        cost_estimate=SMALL,
        name="norm",
    )(own, oth, h1, h2, floor, mix)


def epi_kernel(pieces, v0, v1, has_prev, *refs):
    k = pieces[-1][0] + 1 + pieces[-1][1]
    srcs = refs[:k]
    wm_ref, we_ref, bias_ref = refs[k:k + 3]
    rest = refs[k + 3 + has_prev:]
    out_ref, cod, obuf, sem_in, sem_out = rest
    U = srcs[0].shape[1]
    n, c = cod.shape[2], cod.shape[3]
    V = out_ref.shape[1]
    total = out_ref.shape[0]
    nv = v1 - v0
    for p, (at, parts, s0, s1, d0) in enumerate(pieces):
        for j in range(4):
            src = srcs[at].at[j] if j < 2 else srcs[at + j - 1] if parts > 1 else srcs[at + 1].at[j - 2]
            blk = lax.axis_index("view") ^ (0, 2, 1, 3)[j]
            cp = pltpu.make_async_copy(src.at[:, s0:s1], cod.at[pl.ds(1 + U * blk, U), d0:d0 + s1 - s0], sem_in.at[4 * p + blk])
            cp.start()
    edge = jnp.zeros((nv + 2, n, c), bf16)
    cod[0] = edge
    cod[total + 1] = edge
    if v0 == 0:
        cod[:, 0] = jnp.zeros((total + 2, n, c), bf16)
    if v1 == V:
        cod[:, nv + 1] = jnp.zeros((total + 2, n, c), bf16)

    def arrived(b):
        for p, (at, parts, s0, s1, d0) in enumerate(pieces):
            pltpu.make_async_copy(
                srcs[at].at[0, :, s0:s1], cod.at[1 + U * b:1 + U * (b + 1), d0:d0 + s1 - s0], sem_in.at[4 * p + b]
            ).wait()
    m = nv * n
    steps = total // 2
    def out_copy(t, slot):
        return pltpu.make_async_copy(obuf.at[slot], out_ref.at[pl.ds(2 * t, 2), v0:v1, 0], sem_out.at[slot])
    def step(t, carry):
        slot = lax.rem(t, 2)
        for b in range(total // U):
            pl.when(t == max(0, -(-(U * b - 2) // 2)))(functools.partial(arrived, b))

        @pl.when(t >= 2)
        def _():
            out_copy(t - 2, slot).wait()
        def block(i, j):
            return cod[2 * t + i, j:j + nv].reshape(m, c)
        blocks = [[block(i, j) for j in range(3)] for i in range(4)]
        ex = jnp.dot(jnp.concatenate(sum(blocks, []), axis=1), we_ref[...], preferred_element_type=f32)
        for h in range(2):
            mn = jnp.dot(jnp.concatenate(sum(blocks[h:h + 3], []), axis=1), wm_ref[...], preferred_element_type=f32)
            res = shifted_sum(mn[:, :c], mn[:, c:], ex[:, h * c:(h + 1) * c], n) + bias_ref[...]
            obuf[slot, h] = res.astype(bf16).reshape(nv, n, c)
        out_copy(t, slot).start()
        return carry
    lax.fori_loop(0, steps, step, 0)
    for t in (steps - 2, steps - 1):
        out_copy(t, t % 2).wait()

def epi_weights(k):
    c = k.shape[3]
    main = jnp.concatenate([k[:, :, 0], k[:, :, 1]], -1).reshape(-1, 2 * c)
    z = jnp.zeros((1,) + k.shape[1:2] + k.shape[3:], k.dtype)
    last = jnp.concatenate([jnp.concatenate([k[:, :, 2], z], 0), jnp.concatenate([z, k[:, :, 2]], 0)], -1)
    return main, last.reshape(-1, 2 * c)

def epi_chunk(sources, spans, v0, v1, prev, wm, we, bias, total, V):
    used, pieces = [], []
    for (mine, flipped), (lo, hi) in zip(sources, spans):
        a, b = max(lo, v0 - 1), min(hi, v1 + 1)
        if a < b:
            pieces.append((len(used), len(flipped), a - lo, b - lo, a - (v0 - 1)))
            used += [mine, *flipped]
    _, U, _, n, C = used[0].shape
    anyspec = pl.BlockSpec(memory_space=pl.ANY)
    whole = pl.BlockSpec(memory_space=pltpu.VMEM)
    nv = v1 - v0
    args = used + [wm, we, bias] + ([prev] if prev is not None else [])
    return pl.pallas_call(
        functools.partial(epi_kernel, tuple(pieces), v0, v1, int(prev is not None)),
        grid=(1,),
        in_specs=[anyspec] * len(used) + [whole] * 3 + [anyspec] * (prev is not None),
        out_specs=anyspec,
        scratch_shapes=[
            pltpu.VMEM((total + 2, nv + 2, n, C), bf16),
            pltpu.VMEM((2, 2, nv, n, C), bf16),
            pltpu.SemaphoreType.DMA((4 * len(pieces),)),
            pltpu.SemaphoreType.DMA((2,)),
        ],
        out_shape=jax.ShapeDtypeStruct((total, V, 1, n, C), bf16),
        input_output_aliases={len(args) - 1: 0} if prev is not None else {},
        compiler_params=pltpu.CompilerParams(vmem_limit_bytes=24 * 2**20),
        cost_estimate=SMALL,
        name="epi",
    )(*args)


CHUNKS = ((0, 4), (4, 9), (9, 12))
PARTS = (1, 2, 1)


def shards(features, analysis_kernel, norm_floor, norm_mixing, epipolar_kernel, epipolar_bias):
    U, V = features.shape[:2]
    views, bands = lax.axis_size("view"), lax.axis_size("rows")
    total = U * views
    em, ee = epi_weights(epipolar_kernel)
    floor, bias = norm_floor[None], epipolar_bias[None]
    both = ("view", "rows")
    swap = [(v * bands + r, (v ^ 2) * bands + r) for v in range(views) for r in range(bands)]
    def hop(flip):
        pairs = []
        for v in range(views):
            step = 1 if (v < 2) != (flip > 0) else -1
            pairs += [(v * bands + r, (v ^ flip) * bands + r + step) for r in range(bands) if 0 <= r + step < bands]
        return pairs
    core = [(v, v ^ 1) for v in range(views)]
    h1_sum, h2_sum, wm, we = halo_sums(features, analysis_kernel)
    h1 = lax.ppermute(h1_sum, both, hop(0))
    h2 = lax.ppermute(h2_sum, both, hop(2))
    rows, sent = [], []
    features, last = lax.optimization_barrier((features, h1_sum))
    for spans in (CHUNKS[:1], CHUNKS[1:]):
        done = conv_chunks(features, wm, we, spans)
        rows += done[::2]
        sent += done[1::2]
        features, last = lax.optimization_barrier((features, done[0]))
    sent[0] = lax.ppermute(sent[0], both, swap)
    sent[1], h1, h2 = lax.optimization_barrier((sent[1], h1, h2))
    sent[1] = lax.ppermute(sent[1], both, swap)
    sources = []
    out = None
    done = 0
    for i, (lo, hi) in enumerate(CHUNKS):
        own, oth = rows[i], sent[i]
        if out is None:
            oth, rows[-1] = lax.optimization_barrier((oth, rows[-1]))
        else:
            oth, out = lax.optimization_barrier((oth, out))
        mine, *give = norm_chunk(own, oth, h1, h2, floor, norm_mixing, lo, PARTS[i])
        flipped = [lax.ppermute(g, "view", core) for g in give]
        sources.append((mine, flipped))
        upto = V if hi == V else hi - 1
        out = epi_chunk(sources, CHUNKS[:i + 1], done, upto, out, em, ee, bias, total, V)
        done = upto
        if i + 2 < len(CHUNKS):
            sent[i + 2], out = lax.optimization_barrier((sent[i + 2], out))
            sent[i + 2] = lax.ppermute(sent[i + 2], both, swap)
    return out


def solution(mesh):
    in_specs = (P("view", None, "rows", None, None), P(), P(), P(), P(), P())
    out_specs = P(None, None, ("rows", "view"), None, None)
    return jax.shard_map(shards, mesh=mesh, in_specs=in_specs, out_specs=out_specs, check_vma=False)
```

```python
import functools
import jax, jax.numpy as jnp
from jax import lax
from jax.experimental import pallas as pl
from jax.experimental.pallas import tpu as pltpu
from jax.sharding import PartitionSpec as P

bf16, f32 = jnp.bfloat16, jnp.float32

SMALL = pl.CostEstimate(flops=1000, bytes_accessed=1000, transcendentals=0)


def shifted_sum(before, here, after, cols):
    rows = before.shape[0]
    place = lax.broadcasted_iota(jnp.int32, before.shape, 0) % cols
    down = jnp.where(place == 0, 0.0, pltpu.roll(before, 1, 0))
    up = jnp.where(place == cols - 1, 0.0, pltpu.roll(after, rows - 1, 0))
    return down + here + up

def split_columns(x_ref, v, i, wide, ev, od, at):
    n = wide.shape[1] // 2
    wide[at] = x_ref[v, i].astype(f32)
    ev[v, at] = wide[at, pl.ds(0, n, 2), :].astype(bf16)
    od[v, at] = wide[at, pl.ds(1, n, 2), :].astype(bf16)


def main_weights(k_ref, wm_ref):
    c = k_ref.shape[2]
    for a in range(5):
        for p in range(2):
            for s in range(2):
                wm_ref[(2 * a + p) * c:(2 * a + p + 1) * c, s * c:(s + 1) * c] = k_ref[a, 2 * s + p]


def side_blocks(refs, blocks, m):
    return jnp.concatenate([refs[p][:, i].reshape(m, -1) for p, i in blocks], axis=1)


def partial_sums(refs, places, wm_ref, we_ref, h1_ref, h2_ref, b, first):
    g, _, n, c = refs[0].shape
    m = g * n
    top, low, last = places
    up = jnp.dot(side_blocks(refs, [(0, top), (1, top)], m), wm_ref[8 * c:, :], preferred_element_type=f32)
    side = jnp.dot(side_blocks(refs, [(0, top)], m), we_ref[4 * c:5 * c, :c], preferred_element_type=f32)
    up = shifted_sum(up[:, :c], up[:, c:], side, n).astype(bf16).reshape(g, n, c)
    dn = jnp.dot(side_blocks(refs, [(0, low), (1, low), (0, last), (1, last)], m), wm_ref[:4 * c, :], preferred_element_type=f32)
    side = jnp.dot(side_blocks(refs, [(0, low), (0, last)], m), we_ref[:2 * c, :c], preferred_element_type=f32)
    dn = shifted_sum(dn[:, :c], dn[:, c:], side, n).astype(bf16).reshape(g, n, c)
    h1_ref[:, b] = jnp.where(first, dn, up)
    h2_ref[:, b] = jnp.where(first, up, dn)


def conv_kernel(base, starts, x_ref, k_ref, *rest):
    outs, (xs, kern, wide, ev, od, wm_ref, we_ref, sems) = rest[:-8], rest[-8:]
    count, g, rows, wid, c = xs.shape
    n = wid // 2
    m = g * n

    def fetch(b):
        return pltpu.make_async_copy(x_ref.at[:, base + b], xs.at[b], sems.at[b])

    weights = pltpu.make_async_copy(k_ref, kern, sems.at[count])
    weights.start()
    for b in range(count):
        fetch(b).start()
    weights.wait()
    main_weights(kern, wm_ref)
    z = jnp.zeros((c, c), bf16)
    for j in range(7):
        we_ref[j * c:(j + 1) * c, :c] = kern[j, 4] if j < 5 else z
        we_ref[j * c:(j + 1) * c, c:] = kern[j - 2, 4] if j > 1 else z
    first = lax.axis_index("view") < 2
    refs = (ev, od)

    def main(lo, hi, a):
        lhs = side_blocks(refs, [(p, i) for i in range(lo, hi) for p in range(2)], m)
        return jnp.dot(lhs, wm_ref[a * 2 * c:(a + hi - lo) * 2 * c, :], preferred_element_type=f32)

    def side(lo, hi, a):
        lhs = side_blocks(refs, [(0, i) for i in range(lo, hi)], m)
        return jnp.dot(lhs, we_ref[a * c:(a + hi - lo) * c, :], preferred_element_type=f32)

    def row(mn, sd):
        return shifted_sum(mn[:, :c], mn[:, c:], sd, n).astype(bf16).reshape(g, n, c)

    def step(own_ref, oth_ref, start, b, carry):
        fetch(b).wait()
        for v in range(g):
            for i in range(rows):
                split_columns(xs.at[b], v, i, wide, ev, od, i)
        at = b - start
        pair = side(0, 5, 2)
        r0 = row(main(0, 3, 2), pair[:, :c])
        r1 = row(main(0, 5, 0), pair[:, c:])
        pair = side(2, 8, 0)
        r2 = row(main(2, 7, 0), pair[:, :c])
        r3 = row(main(4, 8, 0), pair[:, c:])
        own_ref[0, :, at] = jnp.where(first, r0, r2)
        own_ref[1, :, at] = jnp.where(first, r1, r3)
        oth_ref[0, :, at] = jnp.where(first, r2, r0)
        oth_ref[1, :, at] = jnp.where(first, r3, r1)
        partial_sums(refs, (0, rows - 2, rows - 1), wm_ref, we_ref, outs[-2], outs[-1], b, first)
        return carry

    for q, start in enumerate(starts):
        end = starts[q + 1] if q + 1 < len(starts) else count
        lax.fori_loop(start, end, functools.partial(step, outs[2 * q], outs[2 * q + 1], start), 0)


def conv_chunks(features, kernel, spans, mib):
    U, V, H, W, C = features.shape
    n = W // 2
    base = spans[0][0]
    starts = tuple(lo - base for lo, _ in spans)

    count = spans[-1][1] - base
    whole = pl.BlockSpec(memory_space=pltpu.VMEM)
    return pl.pallas_call(
        functools.partial(conv_kernel, base, starts),
        in_specs=[pl.BlockSpec(memory_space=pl.ANY)] * 2,
        out_specs=[whole] * (2 * len(spans) + 2),
        scratch_shapes=[
            pltpu.VMEM((count, U, H, W, C), bf16), pltpu.VMEM(kernel.shape, bf16),
            pltpu.VMEM((H, W, C), f32), pltpu.VMEM((U, H, n, C), bf16), pltpu.VMEM((U, H, n, C), bf16),
            pltpu.VMEM((10 * C, 2 * C), bf16), pltpu.VMEM((7 * C, 2 * C), bf16),
            pltpu.SemaphoreType.DMA((count + 1,)),
        ],
        out_shape=[jax.ShapeDtypeStruct((2, U, hi - lo, n, C), bf16) for lo, hi in spans for _ in range(2)]
        + [jax.ShapeDtypeStruct((U, count, n, C), bf16)] * 2,
        compiler_params=pltpu.CompilerParams(vmem_limit_bytes=mib * 2**20),
        cost_estimate=SMALL,
        name="conv",
    )(features, kernel)


def norm_kernel(lo, own_ref, oth_ref, h1_ref, h2_ref, floor_ref, mix_ref, mine_ref, *give_refs):
    place = lax.axis_index("view")
    first = place < 2
    upper = place % 2 == 0
    _, g, cv, n, c = own_ref.shape
    mix = mix_ref[...].astype(bf16)

    def step(v, carry):
        for j, (raw_ref, part_ref) in enumerate(((own_ref, h1_ref), (oth_ref, h2_ref))):
            part = part_ref[:, lo + v].reshape(g * n, c).astype(f32)
            coded = []
            for r in range(2):
                x = raw_ref[r, :, v].reshape(g * n, c).astype(f32)
                x = x + jnp.where(first == (r == 0), part, 0.0)
                energy = jnp.dot((x * x).astype(bf16), mix, preferred_element_type=f32)
                coded.append((x * lax.rsqrt(floor_ref[...] + energy)).astype(bf16).reshape(g, n, c))
            mine_ref[j, :, v] = jnp.where(upper, coded[0], coded[1])
            give = give_refs[j] if len(give_refs) > 1 else give_refs[0].at[j]
            give[:, v] = jnp.where(upper, coded[1], coded[0])
        return carry

    lax.fori_loop(0, cv, step, 0)


def norm_chunk(own, oth, h1, h2, floor, mix, lo, parts):
    _, U, cv, n, C = own.shape
    whole = pl.BlockSpec(memory_space=pltpu.VMEM)
    return pl.pallas_call(
        functools.partial(norm_kernel, lo),
        in_specs=[whole] * 6,
        out_specs=[whole] * (1 + parts),
        out_shape=[jax.ShapeDtypeStruct((2, U, cv, n, C), bf16)]
        + [jax.ShapeDtypeStruct((2,) * (2 - parts) + (U, cv, n, C), bf16)] * parts,
        compiler_params=pltpu.CompilerParams(vmem_limit_bytes=16 * 2**20),
        cost_estimate=SMALL,
        name="norm",
    )(own, oth, h1, h2, floor, mix)


def epi_kernel(pieces, v0, v1, has_prev, *refs):
    k = pieces[-1][0] + 1 + pieces[-1][1]
    srcs = refs[:k]
    wm_ref, we_ref, bias_ref = refs[k:k + 3]
    rest = refs[k + 3 + has_prev:]
    out_ref, cod, obuf, sem_in, sem_out = rest
    U = srcs[0].shape[1]
    n, c = cod.shape[2], cod.shape[3]
    V = out_ref.shape[1]
    total = out_ref.shape[0]
    nv = v1 - v0
    for p, (at, parts, s0, s1, d0) in enumerate(pieces):
        for j in range(4):
            src = srcs[at].at[j] if j < 2 else srcs[at + j - 1] if parts > 1 else srcs[at + 1].at[j - 2]
            blk = lax.axis_index("view") ^ (0, 2, 1, 3)[j]
            cp = pltpu.make_async_copy(src.at[:, s0:s1], cod.at[pl.ds(1 + U * blk, U), d0:d0 + s1 - s0], sem_in.at[4 * p + blk])
            cp.start()
    edge = jnp.zeros((nv + 2, n, c), bf16)
    cod[0] = edge
    cod[total + 1] = edge
    if v0 == 0:
        cod[:, 0] = jnp.zeros((total + 2, n, c), bf16)
    if v1 == V:
        cod[:, nv + 1] = jnp.zeros((total + 2, n, c), bf16)

    def arrived(b):
        for p, (at, parts, s0, s1, d0) in enumerate(pieces):
            pltpu.make_async_copy(
                srcs[at].at[0, :, s0:s1], cod.at[1 + U * b:1 + U * (b + 1), d0:d0 + s1 - s0], sem_in.at[4 * p + b]
            ).wait()
    m = nv * n
    steps = total // 2
    def out_copy(t, slot):
        return pltpu.make_async_copy(obuf.at[slot], out_ref.at[pl.ds(2 * t, 2), v0:v1, 0], sem_out.at[slot])
    def step(t, carry):
        slot = lax.rem(t, 2)
        for b in range(total // U):
            pl.when(t == max(0, -(-(U * b - 2) // 2)))(functools.partial(arrived, b))

        @pl.when(t >= 2)
        def _():
            out_copy(t - 2, slot).wait()
        def block(i, j):
            return cod[2 * t + i, j:j + nv].reshape(m, c)
        blocks = [[block(i, j) for j in range(3)] for i in range(4)]
        ex = jnp.dot(jnp.concatenate(sum(blocks, []), axis=1), we_ref[...], preferred_element_type=f32)
        for h in range(2):
            mn = jnp.dot(jnp.concatenate(sum(blocks[h:h + 3], []), axis=1), wm_ref[...], preferred_element_type=f32)
            res = shifted_sum(mn[:, :c], mn[:, c:], ex[:, h * c:(h + 1) * c], n) + bias_ref[...]
            obuf[slot, h] = res.astype(bf16).reshape(nv, n, c)
        out_copy(t, slot).start()
        return carry
    lax.fori_loop(0, steps, step, 0)
    for t in (steps - 2, steps - 1):
        out_copy(t, t % 2).wait()

def epi_weights(k):
    c = k.shape[3]
    main = jnp.concatenate([k[:, :, 0], k[:, :, 1]], -1).reshape(-1, 2 * c)
    z = jnp.zeros((1,) + k.shape[1:2] + k.shape[3:], k.dtype)
    last = jnp.concatenate([jnp.concatenate([k[:, :, 2], z], 0), jnp.concatenate([z, k[:, :, 2]], 0)], -1)
    return main, last.reshape(-1, 2 * c)

def epi_chunk(sources, spans, v0, v1, prev, wm, we, bias, total, V):
    used, pieces = [], []
    for (mine, flipped), (lo, hi) in zip(sources, spans):
        a, b = max(lo, v0 - 1), min(hi, v1 + 1)
        if a < b:
            pieces.append((len(used), len(flipped), a - lo, b - lo, a - (v0 - 1)))
            used += [mine, *flipped]
    _, U, _, n, C = used[0].shape
    anyspec = pl.BlockSpec(memory_space=pl.ANY)
    whole = pl.BlockSpec(memory_space=pltpu.VMEM)
    nv = v1 - v0
    args = used + [wm, we, bias] + ([prev] if prev is not None else [])
    return pl.pallas_call(
        functools.partial(epi_kernel, tuple(pieces), v0, v1, int(prev is not None)),
        grid=(1,),
        in_specs=[anyspec] * len(used) + [whole] * 3 + [anyspec] * (prev is not None),
        out_specs=anyspec,
        scratch_shapes=[
            pltpu.VMEM((total + 2, nv + 2, n, C), bf16),
            pltpu.VMEM((2, 2, nv, n, C), bf16),
            pltpu.SemaphoreType.DMA((4 * len(pieces),)),
            pltpu.SemaphoreType.DMA((2,)),
        ],
        out_shape=jax.ShapeDtypeStruct((total, V, 1, n, C), bf16),
        input_output_aliases={len(args) - 1: 0} if prev is not None else {},
        compiler_params=pltpu.CompilerParams(vmem_limit_bytes=24 * 2**20),
        cost_estimate=SMALL,
        name="epi",
    )(*args)


CHUNKS = ((0, 5), (5, 9), (9, 12))
PARTS = (2, 2, 1)


def shards(features, analysis_kernel, norm_floor, norm_mixing, epipolar_kernel, epipolar_bias):
    U, V = features.shape[:2]
    views, bands = lax.axis_size("view"), lax.axis_size("rows")
    total = U * views
    em, ee = epi_weights(epipolar_kernel)
    floor, bias = norm_floor[None], epipolar_bias[None]
    both = ("view", "rows")
    swap = [(v * bands + r, (v ^ 2) * bands + r) for v in range(views) for r in range(bands)]
    def hop(flip):
        pairs = []
        for v in range(views):
            step = 1 if (v < 2) != (flip > 0) else -1
            pairs += [(v * bands + r, (v ^ flip) * bands + r + step) for r in range(bands) if 0 <= r + step < bands]
        return pairs
    core = [(v, v ^ 1) for v in range(views)]
    cut = CHUNKS[0][1]
    own0, oth0, h1, h2 = conv_chunks(features, analysis_kernel, CHUNKS[:1], 46)
    features, own0 = lax.optimization_barrier((features, own0))
    early = [lax.ppermute(h1, both, hop(0)), lax.ppermute(h2, both, hop(2))]
    oth0 = lax.ppermute(oth0, both, swap)
    own1, oth1, own2, oth2, h1, h2 = conv_chunks(features, analysis_kernel, CHUNKS[1:], 46)
    h1, h2, oth1, *early = lax.optimization_barrier((h1, h2, oth1, *early))
    late = [lax.ppermute(h1, both, hop(0)), lax.ppermute(h2, both, hop(2))]
    oth1 = lax.ppermute(oth1, both, swap)
    rows, sent = [own0, own1, own2], [oth0, oth1, oth2]
    sources = []
    out = None
    done = 0
    for i, (lo, hi) in enumerate(CHUNKS):
        own, oth = rows[i], sent[i]
        if out is None:
            oth, rows[-1] = lax.optimization_barrier((oth, rows[-1]))
        else:
            oth, out = lax.optimization_barrier((oth, out))
        h1, h2 = late if i else early
        mine, *give = norm_chunk(own, oth, h1, h2, floor, norm_mixing, lo - cut if i else 0, PARTS[i])
        flipped = [lax.ppermute(g, "view", core) for g in give]
        sources.append((mine, flipped))
        upto = V if hi == V else hi - 1
        out = epi_chunk(sources, CHUNKS[:i + 1], done, upto, out, em, ee, bias, total, V)
        done = upto
        if i + 2 < len(CHUNKS):
            sent[i + 2], out = lax.optimization_barrier((sent[i + 2], out))
            sent[i + 2] = lax.ppermute(sent[i + 2], both, swap)
    return out


def solution(mesh):
    in_specs = (P("view", None, "rows", None, None), P(), P(), P(), P(), P())
    out_specs = P(None, None, ("rows", "view"), None, None)
    return jax.shard_map(shards, mesh=mesh, in_specs=in_specs, out_specs=out_specs, check_vma=False)
```

```python
import functools
import jax, jax.numpy as jnp
from jax import lax
from jax.experimental import pallas as pl
from jax.experimental.pallas import tpu as pltpu
from jax.sharding import PartitionSpec as P

bf16, f32 = jnp.bfloat16, jnp.float32

SMALL = pl.CostEstimate(flops=1000, bytes_accessed=1000, transcendentals=0)


def shifted_sum(before, here, after, cols):
    rows = before.shape[0]
    place = lax.broadcasted_iota(jnp.int32, before.shape, 0) % cols
    down = jnp.where(place == 0, 0.0, pltpu.roll(before, 1, 0))
    up = jnp.where(place == cols - 1, 0.0, pltpu.roll(after, rows - 1, 0))
    return down + here + up

def split_columns(x_ref, v, i, wide, ev, od, at):
    n = wide.shape[1] // 2
    wide[at] = x_ref[v, i].astype(f32)
    ev[v, at] = wide[at, pl.ds(0, n, 2), :].astype(bf16)
    od[v, at] = wide[at, pl.ds(1, n, 2), :].astype(bf16)


def main_weights(k_ref, wm_ref):
    c = k_ref.shape[2]
    for a in range(5):
        for p in range(2):
            for s in range(2):
                wm_ref[(2 * a + p) * c:(2 * a + p + 1) * c, s * c:(s + 1) * c] = k_ref[a, 2 * s + p]


def side_blocks(refs, blocks, m):
    return jnp.concatenate([refs[p][:, i].reshape(m, -1) for p, i in blocks], axis=1)


def partial_sums(refs, places, wm_ref, we_ref, h1_ref, h2_ref, b, first):
    g, _, n, c = refs[0].shape
    m = g * n
    top, low, last = places
    up = jnp.dot(side_blocks(refs, [(0, top), (1, top)], m), wm_ref[8 * c:, :], preferred_element_type=f32)
    side = jnp.dot(side_blocks(refs, [(0, top)], m), we_ref[4 * c:5 * c, :c], preferred_element_type=f32)
    up = shifted_sum(up[:, :c], up[:, c:], side, n).astype(bf16).reshape(g, n, c)
    dn = jnp.dot(side_blocks(refs, [(0, low), (1, low), (0, last), (1, last)], m), wm_ref[:4 * c, :], preferred_element_type=f32)
    side = jnp.dot(side_blocks(refs, [(0, low), (0, last)], m), we_ref[:2 * c, :c], preferred_element_type=f32)
    dn = shifted_sum(dn[:, :c], dn[:, c:], side, n).astype(bf16).reshape(g, n, c)
    h1_ref[:, b] = jnp.where(first, dn, up)
    h2_ref[:, b] = jnp.where(first, up, dn)


def conv_kernel(base, starts, x_ref, k_ref, *rest):
    outs, (xs, kern, wide, ev, od, wm_ref, we_ref, sems) = rest[:-8], rest[-8:]
    count, g, rows, wid, c = xs.shape
    n = wid // 2
    m = g * n

    def fetch(b):
        return pltpu.make_async_copy(x_ref.at[:, base + b], xs.at[b], sems.at[b])

    weights = pltpu.make_async_copy(k_ref, kern, sems.at[count])
    weights.start()
    for b in range(count):
        fetch(b).start()
    weights.wait()
    main_weights(kern, wm_ref)
    z = jnp.zeros((c, c), bf16)
    for j in range(7):
        we_ref[j * c:(j + 1) * c, :c] = kern[j, 4] if j < 5 else z
        we_ref[j * c:(j + 1) * c, c:] = kern[j - 2, 4] if j > 1 else z
    first = lax.axis_index("view") < 2
    refs = (ev, od)

    def main(lo, hi, a):
        lhs = side_blocks(refs, [(p, i) for i in range(lo, hi) for p in range(2)], m)
        return jnp.dot(lhs, wm_ref[a * 2 * c:(a + hi - lo) * 2 * c, :], preferred_element_type=f32)

    def side(lo, hi, a):
        lhs = side_blocks(refs, [(0, i) for i in range(lo, hi)], m)
        return jnp.dot(lhs, we_ref[a * c:(a + hi - lo) * c, :], preferred_element_type=f32)

    def row(mn, sd):
        return shifted_sum(mn[:, :c], mn[:, c:], sd, n).astype(bf16).reshape(g, n, c)

    def step(own_ref, oth_ref, start, b, carry):
        fetch(b).wait()
        for v in range(g):
            for i in range(rows):
                split_columns(xs.at[b], v, i, wide, ev, od, i)
        at = b - start
        pair = side(0, 5, 2)
        r0 = row(main(0, 3, 2), pair[:, :c])
        r1 = row(main(0, 5, 0), pair[:, c:])
        pair = side(2, 8, 0)
        r2 = row(main(2, 7, 0), pair[:, :c])
        r3 = row(main(4, 8, 0), pair[:, c:])
        own_ref[0, :, at] = jnp.where(first, r0, r2)
        own_ref[1, :, at] = jnp.where(first, r1, r3)
        oth_ref[0, :, at] = jnp.where(first, r2, r0)
        oth_ref[1, :, at] = jnp.where(first, r3, r1)
        partial_sums(refs, (0, rows - 2, rows - 1), wm_ref, we_ref, outs[-2], outs[-1], b, first)
        return carry

    for q, start in enumerate(starts):
        end = starts[q + 1] if q + 1 < len(starts) else count
        lax.fori_loop(start, end, functools.partial(step, outs[2 * q], outs[2 * q + 1], start), 0)


def conv_chunks(features, kernel, spans, mib):
    U, V, H, W, C = features.shape
    n = W // 2
    base = spans[0][0]
    starts = tuple(lo - base for lo, _ in spans)

    count = spans[-1][1] - base
    whole = pl.BlockSpec(memory_space=pltpu.VMEM)
    return pl.pallas_call(
        functools.partial(conv_kernel, base, starts),
        in_specs=[pl.BlockSpec(memory_space=pl.ANY)] * 2,
        out_specs=[whole] * (2 * len(spans) + 2),
        scratch_shapes=[
            pltpu.VMEM((count, U, H, W, C), bf16), pltpu.VMEM(kernel.shape, bf16),
            pltpu.VMEM((H, W, C), f32), pltpu.VMEM((U, H, n, C), bf16), pltpu.VMEM((U, H, n, C), bf16),
            pltpu.VMEM((10 * C, 2 * C), bf16), pltpu.VMEM((7 * C, 2 * C), bf16),
            pltpu.SemaphoreType.DMA((count + 1,)),
        ],
        out_shape=[jax.ShapeDtypeStruct((2, U, hi - lo, n, C), bf16) for lo, hi in spans for _ in range(2)]
        + [jax.ShapeDtypeStruct((U, count, n, C), bf16)] * 2,
        compiler_params=pltpu.CompilerParams(vmem_limit_bytes=mib * 2**20),
        cost_estimate=SMALL,
        name="conv",
    )(features, kernel)


def norm_kernel(lo, own_ref, oth_ref, h1_ref, h2_ref, floor_ref, mix_ref, mine_ref, *give_refs):
    place = lax.axis_index("view")
    first = place < 2
    upper = place % 2 == 0
    _, g, cv, n, c = own_ref.shape
    mix = mix_ref[...].astype(bf16)

    def step(v, carry):
        for j, (raw_ref, part_ref) in enumerate(((own_ref, h1_ref), (oth_ref, h2_ref))):
            part = part_ref[:, lo + v].reshape(g * n, c).astype(f32)
            coded = []
            for r in range(2):
                x = raw_ref[r, :, v].reshape(g * n, c).astype(f32)
                x = x + jnp.where(first == (r == 0), part, 0.0)
                energy = jnp.dot((x * x).astype(bf16), mix, preferred_element_type=f32)
                coded.append((x * lax.rsqrt(floor_ref[...] + energy)).astype(bf16).reshape(g, n, c))
            mine_ref[j, :, v] = jnp.where(upper, coded[0], coded[1])
            give = give_refs[j] if len(give_refs) > 1 else give_refs[0].at[j]
            give[:, v] = jnp.where(upper, coded[1], coded[0])
        return carry

    lax.fori_loop(0, cv, step, 0)


def norm_chunk(own, oth, h1, h2, floor, mix, lo, parts):
    _, U, cv, n, C = own.shape
    whole = pl.BlockSpec(memory_space=pltpu.VMEM)
    return pl.pallas_call(
        functools.partial(norm_kernel, lo),
        in_specs=[whole] * 6,
        out_specs=[whole] * (1 + parts),
        out_shape=[jax.ShapeDtypeStruct((2, U, cv, n, C), bf16)]
        + [jax.ShapeDtypeStruct((2,) * (2 - parts) + (U, cv, n, C), bf16)] * parts,
        compiler_params=pltpu.CompilerParams(vmem_limit_bytes=16 * 2**20),
        cost_estimate=SMALL,
        name="norm",
    )(own, oth, h1, h2, floor, mix)


def epi_kernel(pieces, v0, v1, has_prev, *refs):
    k = pieces[-1][0] + 1 + pieces[-1][1]
    srcs = refs[:k]
    wm_ref, we_ref, bias_ref = refs[k:k + 3]
    rest = refs[k + 3 + has_prev:]
    out_ref, cod, obuf, sem_in, sem_out = rest
    U = srcs[0].shape[1]
    n, c = cod.shape[2], cod.shape[3]
    V = out_ref.shape[1]
    total = out_ref.shape[0]
    nv = v1 - v0
    for p, (at, parts, s0, s1, d0) in enumerate(pieces):
        for j in range(4):
            src = srcs[at].at[j] if j < 2 else srcs[at + j - 1] if parts > 1 else srcs[at + 1].at[j - 2]
            blk = lax.axis_index("view") ^ (0, 2, 1, 3)[j]
            cp = pltpu.make_async_copy(src.at[:, s0:s1], cod.at[pl.ds(1 + U * blk, U), d0:d0 + s1 - s0], sem_in.at[4 * p + blk])
            cp.start()
    edge = jnp.zeros((nv + 2, n, c), bf16)
    cod[0] = edge
    cod[total + 1] = edge
    if v0 == 0:
        cod[:, 0] = jnp.zeros((total + 2, n, c), bf16)
    if v1 == V:
        cod[:, nv + 1] = jnp.zeros((total + 2, n, c), bf16)

    def arrived(b):
        for p, (at, parts, s0, s1, d0) in enumerate(pieces):
            pltpu.make_async_copy(
                srcs[at].at[0, :, s0:s1], cod.at[1 + U * b:1 + U * (b + 1), d0:d0 + s1 - s0], sem_in.at[4 * p + b]
            ).wait()
    m = nv * n
    steps = total // 2
    def out_copy(t, slot):
        return pltpu.make_async_copy(obuf.at[slot], out_ref.at[pl.ds(2 * t, 2), v0:v1, 0], sem_out.at[slot])
    def step(t, carry):
        slot = lax.rem(t, 2)
        for b in range(total // U):
            pl.when(t == max(0, -(-(U * b - 2) // 2)))(functools.partial(arrived, b))

        @pl.when(t >= 2)
        def _():
            out_copy(t - 2, slot).wait()
        def block(i, j):
            return cod[2 * t + i, j:j + nv].reshape(m, c)
        blocks = [[block(i, j) for j in range(3)] for i in range(4)]
        ex = jnp.dot(jnp.concatenate(sum(blocks, []), axis=1), we_ref[...], preferred_element_type=f32)
        for h in range(2):
            mn = jnp.dot(jnp.concatenate(sum(blocks[h:h + 3], []), axis=1), wm_ref[...], preferred_element_type=f32)
            res = shifted_sum(mn[:, :c], mn[:, c:], ex[:, h * c:(h + 1) * c], n) + bias_ref[...]
            obuf[slot, h] = res.astype(bf16).reshape(nv, n, c)
        out_copy(t, slot).start()
        return carry
    lax.fori_loop(0, steps, step, 0)
    for t in (steps - 2, steps - 1):
        out_copy(t, t % 2).wait()

def epi_weights(k):
    c = k.shape[3]
    main = jnp.concatenate([k[:, :, 0], k[:, :, 1]], -1).reshape(-1, 2 * c)
    z = jnp.zeros((1,) + k.shape[1:2] + k.shape[3:], k.dtype)
    last = jnp.concatenate([jnp.concatenate([k[:, :, 2], z], 0), jnp.concatenate([z, k[:, :, 2]], 0)], -1)
    return main, last.reshape(-1, 2 * c)

def epi_chunk(sources, spans, v0, v1, prev, wm, we, bias, total, V):
    used, pieces = [], []
    for (mine, flipped), (lo, hi) in zip(sources, spans):
        a, b = max(lo, v0 - 1), min(hi, v1 + 1)
        if a < b:
            pieces.append((len(used), len(flipped), a - lo, b - lo, a - (v0 - 1)))
            used += [mine, *flipped]
    _, U, _, n, C = used[0].shape
    anyspec = pl.BlockSpec(memory_space=pl.ANY)
    whole = pl.BlockSpec(memory_space=pltpu.VMEM)
    nv = v1 - v0
    args = used + [wm, we, bias] + ([prev] if prev is not None else [])
    return pl.pallas_call(
        functools.partial(epi_kernel, tuple(pieces), v0, v1, int(prev is not None)),
        grid=(1,),
        in_specs=[anyspec] * len(used) + [whole] * 3 + [anyspec] * (prev is not None),
        out_specs=anyspec,
        scratch_shapes=[
            pltpu.VMEM((total + 2, nv + 2, n, C), bf16),
            pltpu.VMEM((2, 2, nv, n, C), bf16),
            pltpu.SemaphoreType.DMA((4 * len(pieces),)),
            pltpu.SemaphoreType.DMA((2,)),
        ],
        out_shape=jax.ShapeDtypeStruct((total, V, 1, n, C), bf16),
        input_output_aliases={len(args) - 1: 0} if prev is not None else {},
        compiler_params=pltpu.CompilerParams(vmem_limit_bytes=24 * 2**20),
        cost_estimate=SMALL,
        name="epi",
    )(*args)


CHUNKS = ((0, 5), (5, 9), (9, 12))
PARTS = (2, 2, 1)


def shards(features, analysis_kernel, norm_floor, norm_mixing, epipolar_kernel, epipolar_bias):
    U, V = features.shape[:2]
    views, bands = lax.axis_size("view"), lax.axis_size("rows")
    total = U * views
    em, ee = epi_weights(epipolar_kernel)
    floor, bias = norm_floor[None], epipolar_bias[None]
    both = ("view", "rows")
    swap = [(v * bands + r, (v ^ 2) * bands + r) for v in range(views) for r in range(bands)]
    def hop(flip):
        pairs = []
        for v in range(views):
            step = 1 if (v < 2) != (flip > 0) else -1
            pairs += [(v * bands + r, (v ^ flip) * bands + r + step) for r in range(bands) if 0 <= r + step < bands]
        return pairs
    core = [(v, v ^ 1) for v in range(views)]
    cut = CHUNKS[0][1]
    own0, oth0, h1, h2 = conv_chunks(features, analysis_kernel, CHUNKS[:1], 46)
    features, own0 = lax.optimization_barrier((features, own0))
    early = [lax.ppermute(h1, both, hop(0)), lax.ppermute(h2, both, hop(2))]
    oth0 = lax.ppermute(oth0, both, swap)
    own1, oth1, own2, oth2, h1, h2 = conv_chunks(features, analysis_kernel, CHUNKS[1:], 46)
    late = [lax.ppermute(h1, both, hop(0)), lax.ppermute(h2, both, hop(2))]
    oth1, *early = lax.optimization_barrier((oth1, *early))
    oth1 = lax.ppermute(oth1, both, swap)
    rows, sent = [own0, own1, own2], [oth0, oth1, oth2]
    sources = []
    out = None
    done = 0
    for i, (lo, hi) in enumerate(CHUNKS):
        own, oth = rows[i], sent[i]
        if out is None:
            oth, rows[-1] = lax.optimization_barrier((oth, rows[-1]))
        else:
            oth, out = lax.optimization_barrier((oth, out))
        h1, h2 = late if i else early
        mine, *give = norm_chunk(own, oth, h1, h2, floor, norm_mixing, lo - cut if i else 0, PARTS[i])
        flipped = [lax.ppermute(g, "view", core) for g in give]
        sources.append((mine, flipped))
        upto = V if hi == V else hi - 1
        out = epi_chunk(sources, CHUNKS[:i + 1], done, upto, out, em, ee, bias, total, V)
        done = upto
        if i + 2 < len(CHUNKS):
            sent[i + 2], out = lax.optimization_barrier((sent[i + 2], out))
            sent[i + 2] = lax.ppermute(sent[i + 2], both, swap)
    return out


def solution(mesh):
    in_specs = (P("view", None, "rows", None, None), P(), P(), P(), P(), P())
    out_specs = P(None, None, ("rows", "view"), None, None)
    return jax.shard_map(shards, mesh=mesh, in_specs=in_specs, out_specs=out_specs, check_vma=False)
```

```python
import functools
import jax, jax.numpy as jnp
from jax import lax
from jax.experimental import pallas as pl
from jax.experimental.pallas import tpu as pltpu
from jax.sharding import PartitionSpec as P

bf16, f32 = jnp.bfloat16, jnp.float32

SMALL = pl.CostEstimate(flops=1000, bytes_accessed=1000, transcendentals=0)


def shifted_sum(before, here, after, cols):
    rows = before.shape[0]
    place = lax.broadcasted_iota(jnp.int32, before.shape, 0) % cols
    down = jnp.where(place == 0, 0.0, pltpu.roll(before, 1, 0))
    up = jnp.where(place == cols - 1, 0.0, pltpu.roll(after, rows - 1, 0))
    return down + here + up

def split_columns(x_ref, v, i, wide, ev, od, at, to):
    n = wide.shape[2] // 2
    wide[to, at] = x_ref[v, i].astype(f32)
    ev[to, at] = wide[to, at, pl.ds(0, n, 2), :].astype(bf16)
    od[to, at] = wide[to, at, pl.ds(1, n, 2), :].astype(bf16)


def main_weights(k_ref, wm_ref):
    c = k_ref.shape[2]
    for a in range(5):
        for p in range(2):
            for s in range(2):
                wm_ref[(2 * a + p) * c:(2 * a + p + 1) * c, s * c:(s + 1) * c] = k_ref[a, 2 * s + p]


def side_blocks(refs, blocks, m):
    return jnp.concatenate([refs[p][:, i].reshape(m, -1) for p, i in blocks], axis=1)


def halo_kernel(x_ref, k_ref, h1_ref, h2_ref, wm_ref, we_ref, top, bottom, kern, wide, ev, od, sems):
    g, views, _, wid, c = top.shape
    rows = x_ref.shape[2]
    n = wid // 2
    m = g * n
    weights = pltpu.make_async_copy(k_ref, kern, sems.at[2 * views])
    weights.start()

    def pieces(b):
        return (
            pltpu.make_async_copy(x_ref.at[:, b, 0:1], top.at[:, b], sems.at[2 * b]),
            pltpu.make_async_copy(x_ref.at[:, b, rows - 2:rows], bottom.at[:, b], sems.at[2 * b + 1]),
        )

    for b in range(views):
        for piece in pieces(b):
            piece.start()
    weights.wait()
    main_weights(kern, wm_ref)
    z = jnp.zeros((c, c), bf16)
    for j in range(7):
        we_ref[j * c:(j + 1) * c, :c] = kern[j, 4] if j < 5 else z
        we_ref[j * c:(j + 1) * c, c:] = kern[j - 2, 4] if j > 1 else z
    first = lax.axis_index("view") < 2
    refs = (ev, od)

    m = HALO_STEP * m

    def step(t, carry):
        for q in range(HALO_STEP):
            b = t * HALO_STEP + q
            for piece in pieces(b):
                piece.wait()
            for v in range(g):
                split_columns(top.at[:, b], v, 0, wide, ev, od, 0, q * g + v)
                split_columns(bottom.at[:, b], v, 0, wide, ev, od, 1, q * g + v)
                split_columns(bottom.at[:, b], v, 1, wide, ev, od, 2, q * g + v)
        up = jnp.dot(side_blocks(refs, [(0, 0), (1, 0)], m), wm_ref[8 * c:, :], preferred_element_type=f32)
        side = jnp.dot(side_blocks(refs, [(0, 0)], m), we_ref[4 * c:5 * c, :c], preferred_element_type=f32)
        up = shifted_sum(up[:, :c], up[:, c:], side, n).astype(bf16).reshape(HALO_STEP, g, n, c)
        dn = jnp.dot(side_blocks(refs, [(0, 1), (1, 1), (0, 2), (1, 2)], m), wm_ref[:4 * c, :], preferred_element_type=f32)
        side = jnp.dot(side_blocks(refs, [(0, 1), (0, 2)], m), we_ref[:2 * c, :c], preferred_element_type=f32)
        dn = shifted_sum(dn[:, :c], dn[:, c:], side, n).astype(bf16).reshape(HALO_STEP, g, n, c)
        for q in range(HALO_STEP):
            b = t * HALO_STEP + q
            h1_ref[:, b] = jnp.where(first, dn[q], up[q])
            h2_ref[:, b] = jnp.where(first, up[q], dn[q])
        return carry

    lax.fori_loop(0, views // HALO_STEP, step, 0)


def halo_sums(features, kernel):
    U, V, H, W, C = features.shape
    n = W // 2
    whole = pl.BlockSpec(memory_space=pltpu.VMEM)
    return pl.pallas_call(
        halo_kernel,
        in_specs=[pl.BlockSpec(memory_space=pl.ANY)] * 2,
        out_specs=[whole] * 4,
        scratch_shapes=[
            pltpu.VMEM((U, V, 1, W, C), bf16), pltpu.VMEM((U, V, 2, W, C), bf16), pltpu.VMEM(kernel.shape, bf16),
            pltpu.VMEM((HALO_STEP * U, 3, W, C), f32),
            pltpu.VMEM((HALO_STEP * U, 3, n, C), bf16), pltpu.VMEM((HALO_STEP * U, 3, n, C), bf16),
            pltpu.SemaphoreType.DMA((2 * V + 1,)),
        ],
        out_shape=[jax.ShapeDtypeStruct((U, V, n, C), bf16)] * 2
        + [jax.ShapeDtypeStruct((taps * C, 2 * C), bf16) for taps in (10, 7)],
        compiler_params=pltpu.CompilerParams(vmem_limit_bytes=57 * 2**20),
        cost_estimate=SMALL,
        name="halo",
    )(features, kernel)


def conv_kernel(base, starts, x_ref, wm_ref, we_ref, *rest):
    outs, (xs, wide, ev, od, sems) = rest[:-5], rest[-5:]
    count, g, rows, wid, c = xs.shape
    n = wid // 2
    m = g * n

    def fetch(b):
        return pltpu.make_async_copy(x_ref.at[:, base + b], xs.at[b], sems.at[b])

    for b in range(count):
        fetch(b).start()
    first = lax.axis_index("view") < 2
    refs = (ev, od)

    def main(lo, hi, a):
        lhs = side_blocks(refs, [(p, i) for i in range(lo, hi) for p in range(2)], m)
        return jnp.dot(lhs, wm_ref[a * 2 * c:(a + hi - lo) * 2 * c, :], preferred_element_type=f32)

    def side(lo, hi, a):
        lhs = side_blocks(refs, [(0, i) for i in range(lo, hi)], m)
        return jnp.dot(lhs, we_ref[a * c:(a + hi - lo) * c, :], preferred_element_type=f32)

    def row(mn, sd):
        return shifted_sum(mn[:, :c], mn[:, c:], sd, n).astype(bf16).reshape(g, n, c)

    def step(own_ref, oth_ref, start, b, carry):
        fetch(b).wait()
        for v in range(g):
            for i in range(rows):
                split_columns(xs.at[b], v, i, wide, ev, od, i, v)
        at = b - start
        pair = side(0, 5, 2)
        r0 = row(main(0, 3, 2), pair[:, :c])
        r1 = row(main(0, 5, 0), pair[:, c:])
        pair = side(2, 8, 0)
        r2 = row(main(2, 7, 0), pair[:, :c])
        r3 = row(main(4, 8, 0), pair[:, c:])
        own_ref[0, :, at] = jnp.where(first, r0, r2)
        own_ref[1, :, at] = jnp.where(first, r1, r3)
        oth_ref[0, :, at] = jnp.where(first, r2, r0)
        oth_ref[1, :, at] = jnp.where(first, r3, r1)
        return carry

    for q, start in enumerate(starts):
        end = starts[q + 1] if q + 1 < len(starts) else count
        lax.fori_loop(start, end, functools.partial(step, outs[2 * q], outs[2 * q + 1], start), 0)


def conv_chunks(features, wm, we, spans):
    U, V, H, W, C = features.shape
    n = W // 2
    base = spans[0][0]
    starts = tuple(lo - base for lo, _ in spans)

    count = spans[-1][1] - base
    whole = pl.BlockSpec(memory_space=pltpu.VMEM)
    return pl.pallas_call(
        functools.partial(conv_kernel, base, starts),
        in_specs=[pl.BlockSpec(memory_space=pl.ANY), whole, whole],
        out_specs=[whole] * (2 * len(spans)),
        scratch_shapes=[
            pltpu.VMEM((count, U, H, W, C), bf16),
            pltpu.VMEM((U, H, W, C), f32), pltpu.VMEM((U, H, n, C), bf16), pltpu.VMEM((U, H, n, C), bf16),
            pltpu.SemaphoreType.DMA((count,)),
        ],
        out_shape=[jax.ShapeDtypeStruct((2, U, hi - lo, n, C), bf16) for lo, hi in spans for _ in range(2)],
        compiler_params=pltpu.CompilerParams(vmem_limit_bytes=46 * 2**20),
        cost_estimate=SMALL,
        name="conv",
    )(features, wm, we)


def norm_kernel(lo, own_ref, oth_ref, h1_ref, h2_ref, floor_ref, mix_ref, mine_ref, *give_refs):
    place = lax.axis_index("view")
    first = place < 2
    upper = place % 2 == 0
    _, g, cv, n, c = own_ref.shape
    mix = mix_ref[...].astype(bf16)

    def step(v, carry):
        for j, (raw_ref, part_ref) in enumerate(((own_ref, h1_ref), (oth_ref, h2_ref))):
            part = part_ref[:, lo + v].reshape(g * n, c).astype(f32)
            coded = []
            for r in range(2):
                x = raw_ref[r, :, v].reshape(g * n, c).astype(f32)
                x = x + jnp.where(first == (r == 0), part, 0.0)
                energy = jnp.dot((x * x).astype(bf16), mix, preferred_element_type=f32)
                coded.append((x * lax.rsqrt(floor_ref[...] + energy)).astype(bf16).reshape(g, n, c))
            mine_ref[j, :, v] = jnp.where(upper, coded[0], coded[1])
            give = give_refs[j] if len(give_refs) > 1 else give_refs[0].at[j]
            give[:, v] = jnp.where(upper, coded[1], coded[0])
        return carry

    lax.fori_loop(0, cv, step, 0)


def norm_chunk(own, oth, h1, h2, floor, mix, lo, parts):
    _, U, cv, n, C = own.shape
    whole = pl.BlockSpec(memory_space=pltpu.VMEM)
    return pl.pallas_call(
        functools.partial(norm_kernel, lo),
        in_specs=[whole] * 6,
        out_specs=[whole] * (1 + parts),
        out_shape=[jax.ShapeDtypeStruct((2, U, cv, n, C), bf16)]
        + [jax.ShapeDtypeStruct((2,) * (2 - parts) + (U, cv, n, C), bf16)] * parts,
        compiler_params=pltpu.CompilerParams(vmem_limit_bytes=16 * 2**20),
        cost_estimate=SMALL,
        name="norm",
    )(own, oth, h1, h2, floor, mix)


def epi_kernel(pieces, v0, v1, has_prev, *refs):
    k = pieces[-1][0] + 1 + pieces[-1][1]
    srcs = refs[:k]
    wm_ref, we_ref, bias_ref = refs[k:k + 3]
    rest = refs[k + 3 + has_prev:]
    out_ref, cod, obuf, sem_in, sem_out = rest
    U = srcs[0].shape[1]
    n, c = cod.shape[2], cod.shape[3]
    V = out_ref.shape[1]
    total = out_ref.shape[0]
    nv = v1 - v0
    for p, (at, parts, s0, s1, d0) in enumerate(pieces):
        for j in range(4):
            src = srcs[at].at[j] if j < 2 else srcs[at + j - 1] if parts > 1 else srcs[at + 1].at[j - 2]
            blk = lax.axis_index("view") ^ (0, 2, 1, 3)[j]
            cp = pltpu.make_async_copy(src.at[:, s0:s1], cod.at[pl.ds(1 + U * blk, U), d0:d0 + s1 - s0], sem_in.at[4 * p + blk])
            cp.start()
    edge = jnp.zeros((nv + 2, n, c), bf16)
    cod[0] = edge
    cod[total + 1] = edge
    if v0 == 0:
        cod[:, 0] = jnp.zeros((total + 2, n, c), bf16)
    if v1 == V:
        cod[:, nv + 1] = jnp.zeros((total + 2, n, c), bf16)

    def arrived(b):
        for p, (at, parts, s0, s1, d0) in enumerate(pieces):
            pltpu.make_async_copy(
                srcs[at].at[0, :, s0:s1], cod.at[1 + U * b:1 + U * (b + 1), d0:d0 + s1 - s0], sem_in.at[4 * p + b]
            ).wait()
    m = nv * n
    steps = total // 2
    def out_copy(t, slot):
        return pltpu.make_async_copy(obuf.at[slot], out_ref.at[pl.ds(2 * t, 2), v0:v1, 0], sem_out.at[slot])
    def step(t, carry):
        slot = lax.rem(t, 2)
        for b in range(total // U):
            pl.when(t == max(0, -(-(U * b - 2) // 2)))(functools.partial(arrived, b))

        @pl.when(t >= 2)
        def _():
            out_copy(t - 2, slot).wait()
        def block(i, j):
            return cod[2 * t + i, j:j + nv].reshape(m, c)
        blocks = [[block(i, j) for j in range(3)] for i in range(4)]
        ex = jnp.dot(jnp.concatenate(sum(blocks, []), axis=1), we_ref[...], preferred_element_type=f32)
        for h in range(2):
            mn = jnp.dot(jnp.concatenate(sum(blocks[h:h + 3], []), axis=1), wm_ref[...], preferred_element_type=f32)
            res = shifted_sum(mn[:, :c], mn[:, c:], ex[:, h * c:(h + 1) * c], n) + bias_ref[...]
            obuf[slot, h] = res.astype(bf16).reshape(nv, n, c)
        out_copy(t, slot).start()
        return carry
    lax.fori_loop(0, steps, step, 0)
    for t in (steps - 2, steps - 1):
        out_copy(t, t % 2).wait()

def epi_weights(k):
    c = k.shape[3]
    main = jnp.concatenate([k[:, :, 0], k[:, :, 1]], -1).reshape(-1, 2 * c)
    z = jnp.zeros((1,) + k.shape[1:2] + k.shape[3:], k.dtype)
    last = jnp.concatenate([jnp.concatenate([k[:, :, 2], z], 0), jnp.concatenate([z, k[:, :, 2]], 0)], -1)
    return main, last.reshape(-1, 2 * c)

def epi_chunk(sources, spans, v0, v1, prev, wm, we, bias, total, V):
    used, pieces = [], []
    for (mine, flipped), (lo, hi) in zip(sources, spans):
        a, b = max(lo, v0 - 1), min(hi, v1 + 1)
        if a < b:
            pieces.append((len(used), len(flipped), a - lo, b - lo, a - (v0 - 1)))
            used += [mine, *flipped]
    _, U, _, n, C = used[0].shape
    anyspec = pl.BlockSpec(memory_space=pl.ANY)
    whole = pl.BlockSpec(memory_space=pltpu.VMEM)
    nv = v1 - v0
    args = used + [wm, we, bias] + ([prev] if prev is not None else [])
    return pl.pallas_call(
        functools.partial(epi_kernel, tuple(pieces), v0, v1, int(prev is not None)),
        grid=(1,),
        in_specs=[anyspec] * len(used) + [whole] * 3 + [anyspec] * (prev is not None),
        out_specs=anyspec,
        scratch_shapes=[
            pltpu.VMEM((total + 2, nv + 2, n, C), bf16),
            pltpu.VMEM((2, 2, nv, n, C), bf16),
            pltpu.SemaphoreType.DMA((4 * len(pieces),)),
            pltpu.SemaphoreType.DMA((2,)),
        ],
        out_shape=jax.ShapeDtypeStruct((total, V, 1, n, C), bf16),
        input_output_aliases={len(args) - 1: 0} if prev is not None else {},
        compiler_params=pltpu.CompilerParams(vmem_limit_bytes=24 * 2**20),
        cost_estimate=SMALL,
        name="epi",
    )(*args)


CHUNKS = ((0, 5), (5, 9), (9, 12))
PARTS = (2, 2, 1)
HALO_STEP = 4


def shards(features, analysis_kernel, norm_floor, norm_mixing, epipolar_kernel, epipolar_bias):
    U, V = features.shape[:2]
    views, bands = lax.axis_size("view"), lax.axis_size("rows")
    total = U * views
    em, ee = epi_weights(epipolar_kernel)
    floor, bias = norm_floor[None], epipolar_bias[None]
    both = ("view", "rows")
    swap = [(v * bands + r, (v ^ 2) * bands + r) for v in range(views) for r in range(bands)]
    def hop(flip):
        pairs = []
        for v in range(views):
            step = 1 if (v < 2) != (flip > 0) else -1
            pairs += [(v * bands + r, (v ^ flip) * bands + r + step) for r in range(bands) if 0 <= r + step < bands]
        return pairs
    core = [(v, v ^ 1) for v in range(views)]
    h1_sum, h2_sum, wm, we = halo_sums(features, analysis_kernel)
    h1 = lax.ppermute(h1_sum, both, hop(0))
    h2 = lax.ppermute(h2_sum, both, hop(2))
    rows, sent = [], []
    features, last = lax.optimization_barrier((features, h1_sum))
    for spans in (CHUNKS[:1], CHUNKS[1:]):
        done = conv_chunks(features, wm, we, spans)
        rows += done[::2]
        sent += done[1::2]
        features, last = lax.optimization_barrier((features, done[0]))
    sent = [lax.ppermute(oth, both, swap) for oth in sent]
    sources = []
    out = None
    done = 0
    for i, (lo, hi) in enumerate(CHUNKS):
        own, oth = rows[i], sent[i]
        if out is None:
            oth, rows[-1] = lax.optimization_barrier((oth, rows[-1]))
        else:
            oth, out = lax.optimization_barrier((oth, out))
        mine, *give = norm_chunk(own, oth, h1, h2, floor, norm_mixing, lo, PARTS[i])
        flipped = [lax.ppermute(g, "view", core) for g in give]
        sources.append((mine, flipped))
        upto = V if hi == V else hi - 1
        out = epi_chunk(sources, CHUNKS[:i + 1], done, upto, out, em, ee, bias, total, V)
        done = upto
    return out


def solution(mesh):
    in_specs = (P("view", None, "rows", None, None), P(), P(), P(), P(), P())
    out_specs = P(None, None, ("rows", "view"), None, None)
    return jax.shard_map(shards, mesh=mesh, in_specs=in_specs, out_specs=out_specs, check_vma=False)
```

```python
import functools
import jax, jax.numpy as jnp
from jax import lax
from jax.experimental import pallas as pl
from jax.experimental.pallas import tpu as pltpu
from jax.sharding import PartitionSpec as P

bf16, f32 = jnp.bfloat16, jnp.float32

SMALL = pl.CostEstimate(flops=1000, bytes_accessed=1000, transcendentals=0)


def shifted_sum(before, here, after, cols):
    rows = before.shape[0]
    place = lax.broadcasted_iota(jnp.int32, before.shape, 0) % cols
    down = jnp.where(place == 0, 0.0, pltpu.roll(before, 1, 0))
    up = jnp.where(place == cols - 1, 0.0, pltpu.roll(after, rows - 1, 0))
    return down + here + up

def split_columns(x_ref, v, i, wide, ev, od, at, to):
    n = wide.shape[2] // 2
    wide[to, at] = x_ref[v, i].astype(f32)
    ev[to, at] = wide[to, at, pl.ds(0, n, 2), :].astype(bf16)
    od[to, at] = wide[to, at, pl.ds(1, n, 2), :].astype(bf16)


def main_weights(k_ref, wm_ref):
    c = k_ref.shape[2]
    for a in range(5):
        for p in range(2):
            for s in range(2):
                wm_ref[(2 * a + p) * c:(2 * a + p + 1) * c, s * c:(s + 1) * c] = k_ref[a, 2 * s + p]


def side_blocks(refs, blocks, m):
    return jnp.concatenate([refs[p][:, i].reshape(m, -1) for p, i in blocks], axis=1)


def halo_kernel(x_ref, k_ref, h1_ref, h2_ref, wm_ref, we_ref, top, bottom, kern, wide, ev, od, sems):
    g, views, _, wid, c = top.shape
    rows = x_ref.shape[2]
    n = wid // 2
    m = g * n
    weights = pltpu.make_async_copy(k_ref, kern, sems.at[2 * views])
    weights.start()

    def pieces(b):
        return (
            pltpu.make_async_copy(x_ref.at[:, b, 0:1], top.at[:, b], sems.at[2 * b]),
            pltpu.make_async_copy(x_ref.at[:, b, rows - 2:rows], bottom.at[:, b], sems.at[2 * b + 1]),
        )

    for b in range(views):
        for piece in pieces(b):
            piece.start()
    weights.wait()
    main_weights(kern, wm_ref)
    z = jnp.zeros((c, c), bf16)
    for j in range(7):
        we_ref[j * c:(j + 1) * c, :c] = kern[j, 4] if j < 5 else z
        we_ref[j * c:(j + 1) * c, c:] = kern[j - 2, 4] if j > 1 else z
    first = lax.axis_index("view") < 2
    refs = (ev, od)

    m = HALO_STEP * m

    def step(t, carry):
        for q in range(HALO_STEP):
            b = t * HALO_STEP + q
            for piece in pieces(b):
                piece.wait()
            for v in range(g):
                split_columns(top.at[:, b], v, 0, wide, ev, od, 0, q * g + v)
                split_columns(bottom.at[:, b], v, 0, wide, ev, od, 1, q * g + v)
                split_columns(bottom.at[:, b], v, 1, wide, ev, od, 2, q * g + v)
        up = jnp.dot(side_blocks(refs, [(0, 0), (1, 0)], m), wm_ref[8 * c:, :], preferred_element_type=f32)
        side = jnp.dot(side_blocks(refs, [(0, 0)], m), we_ref[4 * c:5 * c, :c], preferred_element_type=f32)
        up = shifted_sum(up[:, :c], up[:, c:], side, n).astype(bf16).reshape(HALO_STEP, g, n, c)
        dn = jnp.dot(side_blocks(refs, [(0, 1), (1, 1), (0, 2), (1, 2)], m), wm_ref[:4 * c, :], preferred_element_type=f32)
        side = jnp.dot(side_blocks(refs, [(0, 1), (0, 2)], m), we_ref[:2 * c, :c], preferred_element_type=f32)
        dn = shifted_sum(dn[:, :c], dn[:, c:], side, n).astype(bf16).reshape(HALO_STEP, g, n, c)
        for q in range(HALO_STEP):
            b = t * HALO_STEP + q
            h1_ref[:, b] = jnp.where(first, dn[q], up[q])
            h2_ref[:, b] = jnp.where(first, up[q], dn[q])
        return carry

    lax.fori_loop(0, views // HALO_STEP, step, 0)


def halo_sums(features, kernel):
    U, V, H, W, C = features.shape
    n = W // 2
    whole = pl.BlockSpec(memory_space=pltpu.VMEM)
    return pl.pallas_call(
        halo_kernel,
        in_specs=[pl.BlockSpec(memory_space=pl.ANY)] * 2,
        out_specs=[whole] * 4,
        scratch_shapes=[
            pltpu.VMEM((U, V, 1, W, C), bf16), pltpu.VMEM((U, V, 2, W, C), bf16), pltpu.VMEM(kernel.shape, bf16),
            pltpu.VMEM((HALO_STEP * U, 3, W, C), f32),
            pltpu.VMEM((HALO_STEP * U, 3, n, C), bf16), pltpu.VMEM((HALO_STEP * U, 3, n, C), bf16),
            pltpu.SemaphoreType.DMA((2 * V + 1,)),
        ],
        out_shape=[jax.ShapeDtypeStruct((U, V, n, C), bf16)] * 2
        + [jax.ShapeDtypeStruct((taps * C, 2 * C), bf16) for taps in (10, 7)],
        compiler_params=pltpu.CompilerParams(vmem_limit_bytes=57 * 2**20),
        cost_estimate=SMALL,
        name="halo",
    )(features, kernel)


def conv_kernel(base, starts, x_ref, wm_ref, we_ref, *rest):
    outs, (xs, wide, ev, od, sems) = rest[:-5], rest[-5:]
    count, g, rows, wid, c = xs.shape
    n = wid // 2
    m = g * n

    def fetch(b):
        return pltpu.make_async_copy(x_ref.at[:, base + b], xs.at[b], sems.at[b])

    for b in range(count):
        fetch(b).start()
    first = lax.axis_index("view") < 2
    refs = (ev, od)

    def main(lo, hi, a):
        lhs = side_blocks(refs, [(p, i) for i in range(lo, hi) for p in range(2)], m)
        return jnp.dot(lhs, wm_ref[a * 2 * c:(a + hi - lo) * 2 * c, :], preferred_element_type=f32)

    def side(lo, hi, a):
        lhs = side_blocks(refs, [(0, i) for i in range(lo, hi)], m)
        return jnp.dot(lhs, we_ref[a * c:(a + hi - lo) * c, :], preferred_element_type=f32)

    def row(mn, sd):
        return shifted_sum(mn[:, :c], mn[:, c:], sd, n).astype(bf16).reshape(g, n, c)

    def step(own_ref, oth_ref, start, b, carry):
        fetch(b).wait()
        for v in range(g):
            for i in range(rows):
                split_columns(xs.at[b], v, i, wide, ev, od, i, v)
        at = b - start
        pair = side(0, 5, 2)
        r0 = row(main(0, 3, 2), pair[:, :c])
        r1 = row(main(0, 5, 0), pair[:, c:])
        pair = side(2, 8, 0)
        r2 = row(main(2, 7, 0), pair[:, :c])
        r3 = row(main(4, 8, 0), pair[:, c:])
        own_ref[0, :, at] = jnp.where(first, r0, r2)
        own_ref[1, :, at] = jnp.where(first, r1, r3)
        oth_ref[0, :, at] = jnp.where(first, r2, r0)
        oth_ref[1, :, at] = jnp.where(first, r3, r1)
        return carry

    for q, start in enumerate(starts):
        end = starts[q + 1] if q + 1 < len(starts) else count
        lax.fori_loop(start, end, functools.partial(step, outs[2 * q], outs[2 * q + 1], start), 0)


def conv_chunks(features, wm, we, spans):
    U, V, H, W, C = features.shape
    n = W // 2
    base = spans[0][0]
    starts = tuple(lo - base for lo, _ in spans)

    count = spans[-1][1] - base
    whole = pl.BlockSpec(memory_space=pltpu.VMEM)
    return pl.pallas_call(
        functools.partial(conv_kernel, base, starts),
        in_specs=[pl.BlockSpec(memory_space=pl.ANY), whole, whole],
        out_specs=[whole] * (2 * len(spans)),
        scratch_shapes=[
            pltpu.VMEM((count, U, H, W, C), bf16),
            pltpu.VMEM((U, H, W, C), f32), pltpu.VMEM((U, H, n, C), bf16), pltpu.VMEM((U, H, n, C), bf16),
            pltpu.SemaphoreType.DMA((count,)),
        ],
        out_shape=[jax.ShapeDtypeStruct((2, U, hi - lo, n, C), bf16) for lo, hi in spans for _ in range(2)],
        compiler_params=pltpu.CompilerParams(vmem_limit_bytes=46 * 2**20),
        cost_estimate=SMALL,
        name="conv",
    )(features, wm, we)


def norm_kernel(lo, own_ref, oth_ref, h1_ref, h2_ref, floor_ref, mix_ref, mine_ref, *give_refs):
    place = lax.axis_index("view")
    first = place < 2
    upper = place % 2 == 0
    _, g, cv, n, c = own_ref.shape
    mix = mix_ref[...].astype(bf16)

    def step(v, carry):
        for j, (raw_ref, part_ref) in enumerate(((own_ref, h1_ref), (oth_ref, h2_ref))):
            part = part_ref[:, lo + v].reshape(g * n, c).astype(f32)
            coded = []
            for r in range(2):
                x = raw_ref[r, :, v].reshape(g * n, c).astype(f32)
                x = x + jnp.where(first == (r == 0), part, 0.0)
                energy = jnp.dot((x * x).astype(bf16), mix, preferred_element_type=f32)
                coded.append((x * lax.rsqrt(floor_ref[...] + energy)).astype(bf16).reshape(g, n, c))
            mine_ref[j, :, v] = jnp.where(upper, coded[0], coded[1])
            give = give_refs[j] if len(give_refs) > 1 else give_refs[0].at[j]
            give[:, v] = jnp.where(upper, coded[1], coded[0])
        return carry

    lax.fori_loop(0, cv, step, 0)


def norm_chunk(own, oth, h1, h2, floor, mix, lo, parts):
    _, U, cv, n, C = own.shape
    whole = pl.BlockSpec(memory_space=pltpu.VMEM)
    return pl.pallas_call(
        functools.partial(norm_kernel, lo),
        in_specs=[whole] * 6,
        out_specs=[whole] * (1 + parts),
        out_shape=[jax.ShapeDtypeStruct((2, U, cv, n, C), bf16)]
        + [jax.ShapeDtypeStruct((2,) * (2 - parts) + (U, cv, n, C), bf16)] * parts,
        compiler_params=pltpu.CompilerParams(vmem_limit_bytes=16 * 2**20),
        cost_estimate=SMALL,
        name="norm",
    )(own, oth, h1, h2, floor, mix)


def epi_kernel(pieces, v0, v1, has_prev, *refs):
    k = pieces[-1][0] + 1 + pieces[-1][1]
    srcs = refs[:k]
    wm_ref, we_ref, bias_ref = refs[k:k + 3]
    rest = refs[k + 3 + has_prev:]
    out_ref, cod, obuf, sem_in, sem_out = rest
    U = srcs[0].shape[1]
    n, c = cod.shape[2], cod.shape[3]
    V = out_ref.shape[1]
    total = out_ref.shape[0]
    nv = v1 - v0
    for p, (at, parts, s0, s1, d0) in enumerate(pieces):
        for j in range(4):
            src = srcs[at].at[j] if j < 2 else srcs[at + j - 1] if parts > 1 else srcs[at + 1].at[j - 2]
            blk = lax.axis_index("view") ^ (0, 2, 1, 3)[j]
            cp = pltpu.make_async_copy(src.at[:, s0:s1], cod.at[pl.ds(1 + U * blk, U), d0:d0 + s1 - s0], sem_in.at[4 * p + blk])
            cp.start()
    edge = jnp.zeros((nv + 2, n, c), bf16)
    cod[0] = edge
    cod[total + 1] = edge
    if v0 == 0:
        cod[:, 0] = jnp.zeros((total + 2, n, c), bf16)
    if v1 == V:
        cod[:, nv + 1] = jnp.zeros((total + 2, n, c), bf16)

    def arrived(b):
        for p, (at, parts, s0, s1, d0) in enumerate(pieces):
            pltpu.make_async_copy(
                srcs[at].at[0, :, s0:s1], cod.at[1 + U * b:1 + U * (b + 1), d0:d0 + s1 - s0], sem_in.at[4 * p + b]
            ).wait()
    m = nv * n
    steps = total // 2
    def out_copy(t, slot, h):
        return pltpu.make_async_copy(obuf.at[slot, h], out_ref.at[2 * t + h, v0:v1, 0], sem_out.at[slot, h])
    def step(t, carry):
        slot = lax.rem(t, 2)
        for b in range(total // U):
            pl.when(t == max(0, -(-(U * b - 2) // 2)))(functools.partial(arrived, b))

        @pl.when(t >= 2)
        def _():
            for h in range(2):
                out_copy(t - 2, slot, h).wait()
        def block(i, j):
            return cod[2 * t + i, j:j + nv].reshape(m, c)
        blocks = [[block(i, j) for j in range(3)] for i in range(4)]
        ex = jnp.dot(jnp.concatenate(sum(blocks, []), axis=1), we_ref[...], preferred_element_type=f32)
        for h in range(2):
            mn = jnp.dot(jnp.concatenate(sum(blocks[h:h + 3], []), axis=1), wm_ref[...], preferred_element_type=f32)
            res = shifted_sum(mn[:, :c], mn[:, c:], ex[:, h * c:(h + 1) * c], n) + bias_ref[...]
            obuf[slot, h] = res.astype(bf16).reshape(nv, n, c)
            out_copy(t, slot, h).start()
        return carry
    lax.fori_loop(0, steps, step, 0)
    for t in (steps - 2, steps - 1):
        for h in range(2):
            out_copy(t, t % 2, h).wait()

def epi_weights(k):
    c = k.shape[3]
    main = jnp.concatenate([k[:, :, 0], k[:, :, 1]], -1).reshape(-1, 2 * c)
    z = jnp.zeros((1,) + k.shape[1:2] + k.shape[3:], k.dtype)
    last = jnp.concatenate([jnp.concatenate([k[:, :, 2], z], 0), jnp.concatenate([z, k[:, :, 2]], 0)], -1)
    return main, last.reshape(-1, 2 * c)

def epi_chunk(sources, spans, v0, v1, prev, wm, we, bias, total, V):
    used, pieces = [], []
    for (mine, flipped), (lo, hi) in zip(sources, spans):
        a, b = max(lo, v0 - 1), min(hi, v1 + 1)
        if a < b:
            pieces.append((len(used), len(flipped), a - lo, b - lo, a - (v0 - 1)))
            used += [mine, *flipped]
    _, U, _, n, C = used[0].shape
    anyspec = pl.BlockSpec(memory_space=pl.ANY)
    whole = pl.BlockSpec(memory_space=pltpu.VMEM)
    nv = v1 - v0
    args = used + [wm, we, bias] + ([prev] if prev is not None else [])
    return pl.pallas_call(
        functools.partial(epi_kernel, tuple(pieces), v0, v1, int(prev is not None)),
        grid=(1,),
        in_specs=[anyspec] * len(used) + [whole] * 3 + [anyspec] * (prev is not None),
        out_specs=anyspec,
        scratch_shapes=[
            pltpu.VMEM((total + 2, nv + 2, n, C), bf16),
            pltpu.VMEM((2, 2, nv, n, C), bf16),
            pltpu.SemaphoreType.DMA((4 * len(pieces),)),
            pltpu.SemaphoreType.DMA((2, 2)),
        ],
        out_shape=jax.ShapeDtypeStruct((total, V, 1, n, C), bf16),
        input_output_aliases={len(args) - 1: 0} if prev is not None else {},
        compiler_params=pltpu.CompilerParams(vmem_limit_bytes=24 * 2**20),
        cost_estimate=SMALL,
        name="epi",
    )(*args)


CHUNKS = ((0, 5), (5, 9), (9, 12))
PARTS = (2, 2, 1)
HALO_STEP = 4


def shards(features, analysis_kernel, norm_floor, norm_mixing, epipolar_kernel, epipolar_bias):
    U, V = features.shape[:2]
    views, bands = lax.axis_size("view"), lax.axis_size("rows")
    total = U * views
    em, ee = epi_weights(epipolar_kernel)
    floor, bias = norm_floor[None], epipolar_bias[None]
    both = ("view", "rows")
    swap = [(v * bands + r, (v ^ 2) * bands + r) for v in range(views) for r in range(bands)]
    def hop(flip):
        pairs = []
        for v in range(views):
            step = 1 if (v < 2) != (flip > 0) else -1
            pairs += [(v * bands + r, (v ^ flip) * bands + r + step) for r in range(bands) if 0 <= r + step < bands]
        return pairs
    core = [(v, v ^ 1) for v in range(views)]
    h1_sum, h2_sum, wm, we = halo_sums(features, analysis_kernel)
    h1 = lax.ppermute(h1_sum, both, hop(0))
    h2 = lax.ppermute(h2_sum, both, hop(2))
    rows, sent = [], []
    features, last = lax.optimization_barrier((features, h1_sum))
    for spans in (CHUNKS[:1], CHUNKS[1:]):
        done = conv_chunks(features, wm, we, spans)
        rows += done[::2]
        sent += done[1::2]
        features, last = lax.optimization_barrier((features, done[0]))
    sent = [lax.ppermute(oth, both, swap) for oth in sent]
    sources = []
    out = None
    done = 0
    for i, (lo, hi) in enumerate(CHUNKS):
        own, oth = rows[i], sent[i]
        if out is None:
            oth, rows[-1] = lax.optimization_barrier((oth, rows[-1]))
        else:
            oth, out = lax.optimization_barrier((oth, out))
        mine, *give = norm_chunk(own, oth, h1, h2, floor, norm_mixing, lo, PARTS[i])
        flipped = [lax.ppermute(g, "view", core) for g in give]
        sources.append((mine, flipped))
        upto = V if hi == V else hi - 1
        out = epi_chunk(sources, CHUNKS[:i + 1], done, upto, out, em, ee, bias, total, V)
        done = upto
    return out


def solution(mesh):
    in_specs = (P("view", None, "rows", None, None), P(), P(), P(), P(), P())
    out_specs = P(None, None, ("rows", "view"), None, None)
    return jax.shard_map(shards, mesh=mesh, in_specs=in_specs, out_specs=out_specs, check_vma=False)
```
